256 devices in a mesh: cache: 32 (over z, x), head: 8 (over y, core).
Axes of the slice: x: 4, y: 4, z: 8, core: 2. Of those that a mesh axis runs over, the one named last changes fastest.
Arguments:
- tokens: bfloat16 [8192, 1024], P('cache', 'head'), may hold values from -6 to 6
- request_user: int32 [32, 1], replicated, may hold values from 0 to 15
- hist_len: int32 [16], replicated, may hold values from 1 to 4096, 40960 in all
- history: bfloat16 [2, 16, 4096, 2048], P(None, None, 'cache', 'head'), may hold values from -6 to 6
- w_in: bfloat16 [2, 1024, 2048], P(None, None, 'head'), may hold values from -0.1875 to 0.1875
- w_out: bfloat16 [2, 1024, 1024], P(None, 'head'), may hold values from -0.1875 to 0.1875
Outputs:
- scored: bfloat16 [8192, 1024], P('cache', 'head')
The draws below stay inside these ranges and needn't reach their ends.
Inputs may be any that keep to these rules, and one draw needn't show every extreme that they name: `request_user`: every one of the 16 users is named by at least one request.
All inputs are finite; a program needn't handle non-finite values.
Results may differ from the reference program's by a relative error of at most 0.0095.
Values may be sent and summed in bfloat16 or wider, within the bound.
A program may use at most 64 MiB of HBM per device.

```python
import math
import jax
import jax.numpy as jnp
import numpy as np
from jax import lax

D = 1024
H = 16
DH = 64
LAYERS = 2
CAND = 256
REQUESTS = 32
USERS = 16
HIST = 4096
TOKENS = 8192


def block_levels(rng, extent, shards, smallest, high):
    factor_of, own = 1.0, jax.random.fold_in(rng, 6)
    for axis_at, shards_of in shards:
        draws = jnp.exp(jax.random.uniform(jax.random.fold_in(own, axis_at), (shards_of,), jnp.float32, smallest / len(shards), high / len(shards)))
        factor_of = factor_of * jnp.repeat(draws, extent[axis_at] // shards_of).reshape([-1 if axis == axis_at else 1 for axis in range(len(extent))])
    return factor_of


def different_ones(stream_key, rows, amount, top, lift):
    ranking = jax.random.permutation(jax.random.fold_in(stream_key, 1), amount)
    boost = ranking
    for power in range(3):
        boost = boost * boost // amount
    boost = boost * lift // amount
    lots = jax.random.randint(jax.random.fold_in(stream_key, 2), (rows, amount), 0, 4096) + boost
    sure = jax.random.permutation(jax.random.fold_in(stream_key, 3), rows)[jnp.arange(amount) % rows]
    lots = jnp.where(jnp.arange(rows)[:, None] == sure[None, :], 1 << 14, lots)
    merit = lots * amount + jnp.arange(amount)
    return lax.top_k(merit.astype(jnp.int32), top)[1].astype(jnp.int32)


def split_up(amount, total, bound, slope):
    loads = [(1 << 20) // math.isqrt(rank ** slope) + 1 for rank in range(2, amount + 1)]
    rest, given = total - bound - (amount - 1), [1] * (amount - 1)
    while rest > 0:
        candidates = [i for i in range(amount - 1) if given[i] < bound]
        pool, budget = sum([loads[i] for i in candidates]), rest
        for i in candidates:
            more = min(bound - given[i], max(1, budget * loads[i] // pool), rest)
            given[i] = given[i] + more
            rest = rest - more
    return np.array([bound] + given)


def uneven(rng, amount, total, most, lean):
    if amount == 2:
        one = jax.random.randint(rng, (), max(1, total - most), min(most, total - 1) + 1)
        return jnp.stack([one, total - one])
    lengths = jnp.asarray(split_up(amount, total, most, lean), jnp.int32)
    twos = (amount - 1) // 2
    source_of, taker = lengths[1:1 + 2 * twos:2], lengths[2:2 + 2 * twos:2]
    margin = jnp.minimum(source_of - 1, most - taker)
    shifted = jax.random.randint(jax.random.fold_in(rng, 1), (twos,), 0, 1 << 20) % (margin + 1)
    lengths = lengths.at[1:1 + 2 * twos:2].set(source_of - shifted).at[2:2 + 2 * twos:2].set(taker + shifted)
    return lengths[jax.random.permutation(jax.random.fold_in(rng, 2), amount)]


def scatter_about(stream_key, shape, spread, reach, cuts=(), held_as=jnp.bfloat16):
    entries = spread * jax.random.normal(stream_key, shape, jnp.float32)
    if cuts:
        entries = entries * block_levels(stream_key, shape, cuts, -0.22, 0.18)
    return jnp.clip(entries, -reach, reach).astype(held_as)


def setup_inputs(seed: int = 0) -> dict:
    splits = jax.random.split(jax.random.key(seed), 7)
    return {
        "tokens": scatter_about(splits[0], (TOKENS, D), 1.0, 6.0, ((0, 32), (1, 8))),
        "request_user": different_ones(splits[1], REQUESTS, USERS, 1, 1024),
        "hist_len": uneven(splits[2], USERS, USERS * HIST * 5 // 8, HIST, 2).astype(jnp.int32),
        "history": scatter_about(splits[3], (LAYERS, USERS, HIST, H * 2 * DH), 1.0, 6.0, ((2, 32), (3, 8))),
        "w_in": scatter_about(splits[4], (LAYERS, D, H * 2 * DH), D ** -0.5, 0.1875, ((2, 8),)),
        "w_out": scatter_about(splits[5], (LAYERS, H * DH, D), (H * DH) ** -0.5, 0.1875, ((1, 8),)),
    }


def attend_request(query_rows, history_rows, length):
    blocks = history_rows.reshape(HIST, H, 2, DH)
    key_part = blocks[:, :, 0, :].astype(jnp.float32)
    value_part = blocks[:, :, 1, :].astype(jnp.float32)
    scores = jnp.einsum('chd,ehd->hce', query_rows.astype(jnp.float32), key_part)
    weights = jax.nn.silu(scores * DH ** (-0.5))
    live_mask = jnp.arange(HIST, dtype=jnp.int32) < length
    weights = jnp.where(live_mask[None, None, :], weights, 0.0).astype(jnp.bfloat16)
    return jnp.einsum('hce,ehd->chd', weights.astype(jnp.float32), value_part)

def reference(tokens, request_user, hist_len, history, w_in, w_out):
    user_ids = request_user[:, 0]
    user_lengths = hist_len[user_ids]
    hidden = tokens
    for layer_index in range(LAYERS):
        projected = jnp.dot(hidden, w_in[layer_index], preferred_element_type=jnp.float32)
        projected = projected.reshape(TOKENS, H, 2, DH)
        gate_part = jax.nn.silu(projected[:, :, 0, :]).reshape(TOKENS, H * DH)
        queries = jax.nn.silu(projected[:, :, 1, :]).astype(jnp.bfloat16).reshape(REQUESTS, CAND, H, DH)
        layer_hist = history[layer_index]

        def per_request(packed):
            query_rows, user_one, length = packed
            return attend_request(query_rows, layer_hist[user_one], length)
        attended = lax.map(per_request, (queries, user_ids, user_lengths)).reshape(TOKENS, H * DH)
        row_mean = lax.optimization_barrier(jnp.sum(attended, axis=1)) / (H * DH)
        row_var = lax.optimization_barrier(jnp.sum(attended * attended, axis=1)) / (H * DH) - row_mean * row_mean
        normed = ((attended - row_mean[:, None]) * lax.rsqrt(row_var + 1e-05)[:, None] * gate_part).astype(jnp.bfloat16)
        branch = jnp.dot(normed, w_out[layer_index], preferred_element_type=jnp.float32)
        hidden = (hidden.astype(jnp.float32) + branch).astype(jnp.bfloat16)
    return hidden
```

```python
import functools

import jax
import jax.numpy as jnp
from jax import lax
from jax.experimental import pallas as pl
from jax.experimental.pallas import tpu as pltpu
from jax.sharding import PartitionSpec as P

DH = 64
LAYERS = 2
LANES = 128
X_SIZE = 4
CORES = 2
EXTRA = 16
MESH = pl.DeviceIdType.MESH
F32 = jnp.float32
BF16 = jnp.bfloat16


def dot(a, b, dims=((1,), (0,))):
    return lax.dot_general(a, b, (dims, ((), ())), preferred_element_type=F32)


def silu(v):
    half = v * 0.5
    return half + half * jnp.tanh(half)


def lane_halves(rows):
    return lax.broadcasted_iota(jnp.int32, (rows, LANES), 1) < DH


def head_rows(value, dtype):
    row = lax.broadcasted_iota(jnp.int32, (8, LANES), 0)
    lane = lax.broadcasted_iota(jnp.int32, (8, LANES), 1)
    own = ((row == 0) & (lane < DH)) | ((row == 1) & (lane >= DH))
    return jnp.where(own, value, 0.0).astype(dtype)


def spread(packed):
    flat = jnp.concatenate([packed[0:8], packed[8:16]], axis=1)
    return dot(flat.astype(BF16), head_rows(1.0, BF16), ((0,), (0,)))


def centre(block):
    flat = dot(head_rows(1.0 / DH, BF16), block.astype(BF16), ((1,), (1,)))
    packed = jnp.concatenate([flat[:, 0:LANES], flat[:, LANES:]], axis=0)
    return packed.astype(BF16).astype(F32)


def kernel(
    sizes, req_ref, len_ref, tok_hbm, hist_hbm, w_in_hbm, w_out_hbm, out_ref,
    hist0, hist1, kvs, kvr, hid, hid_f, w_in, wo0, wo_own, wo1, q_all, gate_all, part_s, part_r, att_all,
    load_sem, tok_s, tok_r, kv_s, kv_r, q_s, q_r, g_s, g_r, p_s, p_r, a_s, a_r, wo_s, wo_r, wt_s, wt_r,
):
    nz, nx, nh = sizes
    hists = (hist0, hist1)
    users, events = hist0.shape[0], hist0.shape[1]
    rows = hid.shape[1]
    cache, head = lax.axis_index("cache"), lax.axis_index("head")
    z, x = cache // nx, cache % nx
    core = head % CORES

    def z_peer(d):
        return (((z + d) % nz) * nx + x, head)

    def x_peer(d):
        return (z * nx + (x + d) % nx, head)

    def h_peer(d):
        return (cache, (head + d) % nh)

    def remote(src, dst, send, recv, device):
        return pltpu.make_async_remote_copy(
            src_ref=src, dst_ref=dst, send_sem=send, recv_sem=recv, device_id=device, device_id_type=MESH
        )

    def distance(i):
        return nz // 2 + (1 - 2 * (i % 2)) * ((i + 1) // 2)

    loads = [
        pltpu.make_async_copy(hist_hbm.at[0], hist0, load_sem.at[0]),
        pltpu.make_async_copy(tok_hbm, hid.at[head], load_sem.at[1]),
        pltpu.make_async_copy(w_in_hbm, w_in, load_sem.at[2]),
        pltpu.make_async_copy(w_out_hbm, wo_own, load_sem.at[3]),
        pltpu.make_async_copy(hist_hbm.at[1], hist1, load_sem.at[4]),
    ]
    for load in loads:
        load.start()

    barrier = pltpu.get_barrier_semaphore()
    peers = (
        [z_peer(d) for d in range(1, nz)] + [x_peer(d) for d in range(1, nx)] + [h_peer(d) for d in range(1, nh)]
    )
    for peer in peers:
        pl.semaphore_signal(barrier, inc=1, device_id=peer, device_id_type=MESH)

    def prepare(layer):
        hist = hists[layer]

        def one(u, carry):
            live = len_ref[u] - cache * events
            mask = lax.broadcasted_iota(jnp.int32, (events, LANES), 0) < live
            left = pltpu.roll(hist[u, :, 0:LANES].astype(F32), DH, 1)
            right = hist[u, :, LANES : 2 * LANES].astype(F32)
            hist[u, :, 0:LANES] = jnp.where(mask, left, 0.0).astype(BF16)
            hist[u, :, LANES : 2 * LANES] = jnp.where(mask, right, 0.0).astype(BF16)
            return carry

        lax.fori_loop(0, users, one, 0)

    def gather(layer):
        def one(i, carry):
            z_to = (z + distance(i)) % nz
            for d in range(nx):
                block = hists[layer][req_ref[z_to * nx + (x + d) % nx, 0]]
                if d == 0:
                    kvr[layer, z_to, pl.ds(x * events, events)] = block
                else:
                    kvs[layer, i, d - 1] = block
            return carry

        lax.fori_loop(0, nz, one, 0)

    def kv_copy(layer, i, d):
        z_to = (z + distance(i)) % nz
        return remote(
            kvs.at[layer, i, d - 1], kvr.at[layer, z_to, pl.ds(x * events, events)],
            kv_s.at[layer, i, d - 1], kv_r.at[layer, i, d - 1], x_peer(d),
        )

    def kv_send(layer, i):
        for d in range(1, nx):
            kv_copy(layer, i, d).start()

    def tok_copy(d):
        return remote(hid.at[head], hid.at[head], tok_s.at[d - 1], tok_r.at[d - 1], h_peer(d))

    def wo_peer(d):
        return (cache, (head + CORES * d) % nh)

    def sibling():
        return (cache, head + 1 - 2 * core)

    def wo_copy(d):
        return remote(wo0.at[head], wo0.at[head], wo_s.at[d], wo_r.at[d], wo_peer(d) if d else sibling())

    def wo_forward(d):
        src = (head + nh - CORES * d) % nh
        return remote(wo0.at[src], wo0.at[src], wo_s.at[nh + d], wo_r.at[nh + d], sibling())

    def wt_copy(d):
        to = (head + d) % nh
        return remote(
            wo1.at[1, to], wo1.at[0, head], wt_s.at[d - 1], wt_r.at[d - 1], h_peer(d)
        )

    def q_copy(layer, d):
        return remote(q_all.at[layer, z], q_all.at[layer, z], q_s.at[layer, d], q_r.at[layer, d], z_peer(d))

    def gate_copy(layer, d):
        return remote(
            gate_all.at[layer, head], gate_all.at[layer, head], g_s.at[layer, d - 1], g_r.at[layer, d - 1], h_peer(d)
        )

    def part_copy(layer, i):
        return remote(
            part_s.at[layer, i], part_r.at[layer, i], p_s.at[layer, i], p_r.at[layer, i], z_peer(distance(i))
        )

    def att_copy(layer, d):
        return remote(
            att_all.at[layer, head], att_all.at[layer, head], a_s.at[layer, d - 1], a_r.at[layer, d - 1], h_peer(d)
        )

    loads[0].wait()
    prepare(0)
    gather(0)
    pl.semaphore_wait(barrier, len(peers))
    loads[1].wait()
    for d in range(1, nh):
        tok_copy(d).start()
    lax.fori_loop(0, nz, lambda i, c: (kv_send(0, i), c)[1], 0)

    loads[3].wait()
    wo0[head] = wo_own[0]
    for d in range(nh // CORES):
        wo_copy(d).start()
    for b in range(nh):
        wo1[1, b] = wo_own[1, :, b * LANES : (b + 1) * LANES]
    wo1[0, head] = wo1[1, head]
    for d in range(1, nh):
        wt_copy(d).start()

    loads[4].wait()
    prepare(1)
    gather(1)

    def project(layer):
        if layer == 0:
            for d in range(1, nh):
                tok_copy(d).wait_recv()
            loads[2].wait()
        hidden = jnp.concatenate([hid[b] for b in range(nh)], axis=1)
        left = silu(dot(hidden, w_in[layer, :, 0:LANES]))
        right = pltpu.roll(silu(dot(hidden, w_in[layer, :, LANES : 2 * LANES])), DH, 1)
        low = lane_halves(rows)
        q_all[layer, z] = (jnp.where(low, right, left).astype(BF16).astype(F32) * (0.5 * DH**-0.5)).astype(BF16)
        gate_all[layer, head] = jnp.where(low, left, right).astype(BF16)
        for i in range(nz - 1):
            q_copy(layer, distance(i)).start()
        for d in range(1, nh):
            gate_copy(layer, d).start()

    def attend(layer, z_of):
        q = q_all[layer, z_of]
        low = lane_halves(rows)
        zero = jnp.zeros_like(q)
        outs = []
        for local, q_one in ((0, jnp.where(low, zero, q)), (1, jnp.where(low, q, zero))):
            total = None
            for at in range(0, nx * events, 256):
                kv = kvr[layer, z_of, at : at + 256, local * LANES : (local + 1) * LANES]
                s = dot(q_one, kv, ((1,), (1,)))
                w = (s + s * jnp.tanh(s)).astype(BF16)
                o = dot(w, kv)
                total = o if total is None else total + o
            outs.append(total)
        block = jnp.where(low, outs[0], outs[1])
        centres = centre(block)
        return block - spread(centres), centres

    def attention(layer):
        def one(i, carry):
            d = distance(i)
            q_copy(layer, nz - d).wait_recv()
            for e in range(1, nx):
                kv_copy(layer, i, e).wait_recv()
            block, centres = attend(layer, (z + d) % nz)
            part_s[layer, i, 0:rows] = block.astype(BF16)
            part_s[layer, i, rows : rows + EXTRA] = centres.astype(BF16)
            part_copy(layer, i).start()
            if layer == 0:
                kv_send(1, i)
            return carry

        lax.fori_loop(0, nz - 1, one, 0)
        for e in range(1, nx):
            kv_copy(layer, nz - 1, e).wait_recv()
        if layer == 0:
            kv_send(1, nz - 1)
        block, centres = attend(layer, z)

        def add(i, carry):
            part_copy(layer, i).wait_recv()
            return (
                carry[0] + part_r[layer, i, 0:rows].astype(F32),
                carry[1] + part_r[layer, i, rows : rows + EXTRA].astype(F32),
            )

        for i in range(nz - 1):
            block, centres = add(i, (block, centres))
        high = centres.astype(BF16)
        att_all[layer, head, 0:rows] = block.astype(BF16)
        att_all[layer, head, rows : rows + EXTRA] = high
        att_all[layer, head, rows + EXTRA : rows + 2 * EXTRA] = (centres - high.astype(F32)).astype(BF16)
        for d in range(1, nh):
            att_copy(layer, d).start()

    def normed(layer):
        total = jnp.zeros((rows, LANES), F32)
        squares = jnp.zeros((rows, LANES), F32)
        for d in range(1, nh):
            gate_copy(layer, d).wait_recv()
            att_copy(layer, d).wait_recv()
        for b in range(nh):
            block = (
                att_all[layer, b, 0:rows].astype(F32)
                + spread(att_all[layer, b, rows : rows + EXTRA].astype(F32))
                + spread(att_all[layer, b, rows + EXTRA : rows + 2 * EXTRA].astype(F32))
            )
            hid_f[b] = block
            total = total + block
            squares = squares + block * block
        width = nh * LANES
        mean = jnp.sum(total, axis=1, keepdims=True) * (1.0 / width)
        var = jnp.sum(squares, axis=1, keepdims=True) * (1.0 / width) - mean * mean
        scale = lax.rsqrt(var + 1e-05)
        return jnp.concatenate(
            [((hid_f[b] - mean) * scale * gate_all[layer, b].astype(F32)).astype(BF16) for b in range(nh)], axis=1
        )

    project(0)
    attention(0)
    wo_copy(0).wait_recv()
    for d in range(1, nh // CORES):
        wo_copy(d).wait_recv()
        wo_forward(d).start()
    for d in range(1, nh // CORES):
        wo_forward(d).wait_recv()
    gated = normed(0)
    for d in range(1, nh):
        tok_copy(d).wait_send()
    full = wo0[...].reshape(nh * LANES, nh * LANES)
    for b in range(nh):
        branch = dot(gated, full[:, b * LANES : (b + 1) * LANES])
        hid[b] = (hid[b].astype(F32) + branch).astype(BF16)
    project(1)
    attention(1)
    for d in range(1, nh):
        wt_copy(d).wait_recv()
    gated = normed(1)
    branch = dot(gated, wo1[0].reshape(nh * LANES, LANES))
    out_ref[...] = (hid[head].astype(F32) + branch).astype(BF16)

    for d in range(1, nh):
        wt_copy(d).wait_send()
    for d in range(nh // CORES):
        wo_copy(d).wait_send()
        if d:
            wo_forward(d).wait_send()
    for layer in range(LAYERS):
        for d in range(1, nh):
            gate_copy(layer, d).wait_send()
            att_copy(layer, d).wait_send()

        def finish(i, carry):
            q_copy(layer, distance(i)).wait_send()
            part_copy(layer, i).wait_send()
            for d in range(1, nx):
                kv_copy(layer, i, d).wait_send()
            return carry

        lax.fori_loop(0, nz - 1, finish, 0)
        for d in range(1, nx):
            kv_copy(layer, nz - 1, d).wait_send()


def body(x_size, nc, nh, tokens, request_user, hist_len, history, w_in, w_out):
    nx = x_size
    nz = nc // nx
    rows = tokens.shape[0]
    users, events = history.shape[1], history.shape[2]
    width = nh * LANES
    any_ref = pl.BlockSpec(memory_space=pl.ANY)
    smem = pl.BlockSpec(memory_space=pltpu.SMEM)
    sem = pltpu.SemaphoreType.DMA
    return pl.pallas_call(
        functools.partial(kernel, (nz, nx, nh)),
        out_shape=jax.ShapeDtypeStruct((rows, LANES), BF16),
        in_specs=[smem, smem, any_ref, any_ref, any_ref, any_ref],
        out_specs=pl.BlockSpec(memory_space=pltpu.VMEM),
        scratch_shapes=[
            pltpu.VMEM((users, events, 2 * LANES), BF16),
            pltpu.VMEM((users, events, 2 * LANES), BF16),
            pltpu.VMEM((LAYERS, nz, nx - 1, events, 2 * LANES), BF16),
            pltpu.VMEM((LAYERS, nz, nx * events, 2 * LANES), BF16),
            pltpu.VMEM((nh, rows, LANES), BF16),
            pltpu.VMEM((nh, rows, LANES), F32),
            pltpu.VMEM((LAYERS, width, 2 * LANES), BF16),
            pltpu.VMEM((nh, LANES, width), BF16),
            pltpu.VMEM((LAYERS, LANES, width), BF16),
            pltpu.VMEM((2, nh, LANES, LANES), BF16),
            pltpu.VMEM((LAYERS, nz, rows, LANES), BF16),
            pltpu.VMEM((LAYERS, nh, rows, LANES), BF16),
            pltpu.VMEM((LAYERS, nz, rows + EXTRA, LANES), BF16),
            pltpu.VMEM((LAYERS, nz, rows + EXTRA, LANES), BF16),
            pltpu.VMEM((LAYERS, nh, rows + 2 * EXTRA, LANES), BF16),
            sem((5,)),
            sem((nh,)), sem((nh,)),
            sem((LAYERS, nz, nx)), sem((LAYERS, nz, nx)),
            sem((LAYERS, nz)), sem((LAYERS, nz)),
            sem((LAYERS, nh)), sem((LAYERS, nh)),
            sem((LAYERS, nz)), sem((LAYERS, nz)),
            sem((LAYERS, nh)), sem((LAYERS, nh)),
            sem((2 * nh,)), sem((2 * nh,)),
            sem((nh,)), sem((nh,)),
        ],
        compiler_params=pltpu.CompilerParams(
            collective_id=0, has_side_effects=True, vmem_limit_bytes=48 * 1024 * 1024
        ),
    )(request_user, hist_len, tokens, history, w_in, w_out)


def solution(mesh):
    in_specs = (
        P("cache", "head"),
        P(),
        P(),
        P(None, None, "cache", "head"),
        P(None, None, "head"),
        P(None, "head", None),
    )
    run = functools.partial(body, X_SIZE, mesh.shape["cache"], mesh.shape["head"])
    return jax.shard_map(run, mesh=mesh, in_specs=in_specs, out_specs=P("cache", "head"), check_vma=False)
```

```python
import functools

import jax
import jax.numpy as jnp
from jax import lax
from jax.experimental import pallas as pl
from jax.experimental.pallas import tpu as pltpu
from jax.sharding import PartitionSpec as P

DH = 64
LAYERS = 2
LANES = 128
X_SIZE = 4
CORES = 2
EXTRA = 16
MESH = pl.DeviceIdType.MESH
F32 = jnp.float32
BF16 = jnp.bfloat16


def dot(a, b, dims=((1,), (0,))):
    return lax.dot_general(a, b, (dims, ((), ())), preferred_element_type=F32)


def silu(v):
    half = v * 0.5
    return half + half * jnp.tanh(half)


def lane_halves(rows):
    return lax.broadcasted_iota(jnp.int32, (rows, LANES), 1) < DH


def head_rows(value, dtype):
    row = lax.broadcasted_iota(jnp.int32, (8, LANES), 0)
    lane = lax.broadcasted_iota(jnp.int32, (8, LANES), 1)
    own = ((row == 0) & (lane < DH)) | ((row == 1) & (lane >= DH))
    return jnp.where(own, value, 0.0).astype(dtype)


def spread(flat):
    pick = head_rows(1.0, F32)
    if flat.shape[0] == 16:
        pick = jnp.concatenate([pick, pick], axis=0)
    return dot(flat, pick.astype(BF16), ((0,), (0,)))


def centre(block):
    return dot(head_rows(1.0 / DH, BF16), block.astype(BF16), ((1,), (1,))).astype(BF16)


def kernel(
    sizes, req_ref, len_ref, tok_hbm, hist_hbm, w_in_hbm, w_out_hbm, out_ref,
    raw0, raw1, hist0, hist1, stay_s, stay, pair_s, pair, tok, hid, hid_f, w_in, wo0, wo_own, wo1_s, wo1,
    q_all, gate_s, gate_all, part_s, part_r, att_s, att_all, last_s, last_r,
    load_sem, tok_sem, stay_ss, stay_rs, pair_ss, pair_rs, q_ss, q_rs, p_ss, p_rs, g_ss, g_rs, a_ss, a_rs, wo_sem, wt_sem,
    hid_sem, last_sem,
):
    nz, nx, nh = sizes
    steps = nz // 2
    users, events = raw0.shape[0], raw0.shape[1]
    rows = tok.shape[1]
    half = rows // CORES
    raws, hists = (raw0, raw1), (hist0, hist1)
    cache, head = lax.axis_index("cache"), lax.axis_index("head")
    z, x = cache // nx, cache % nx
    chip, core = head // CORES, head % CORES
    own_rows = pl.ds(pl.multiple_of(core * half, half), half)
    other_rows = pl.ds(pl.multiple_of((1 - core) * half, half), half)
    side = 1 - 2 * (z % 2)
    groups = ((0, 1, 2, 3), (0, 2)) if steps == 4 else (tuple(range(steps)), tuple(range(steps)))
    spans = [steps // len(g) for g in groups]

    def at(d_z, d_x):
        return (((z + d_z + nz) % nz) * nx + (x + d_x) % nx, head)

    def h_peer(d):
        return (cache, (head + d) % nh)

    sibling = (cache, head + 1 - 2 * core)

    def remote(src, dst, send, recv, device):
        return pltpu.make_async_remote_copy(
            src_ref=src, dst_ref=dst, send_sem=send, recv_sem=recv, device_id=device, device_id_type=MESH
        )

    def drain(ref, sem):
        pltpu.make_async_copy(ref, ref, sem).wait()

    loads = [
        pltpu.make_async_copy(hist_hbm.at[0], raw0, load_sem.at[0]),
        pltpu.make_async_copy(tok_hbm, tok.at[head], load_sem.at[1]),
        pltpu.make_async_copy(hist_hbm.at[1], raw1, load_sem.at[2]),
        pltpu.make_async_copy(w_in_hbm, w_in, load_sem.at[3]),
        pltpu.make_async_copy(w_out_hbm, wo_own, load_sem.at[4]),
    ]
    for load in loads:
        load.start()

    barrier = pltpu.get_barrier_semaphore()
    peers = [at(0, d) for d in range(1, nx)] + [h_peer(d) for d in range(1, nh)]
    peers += [at(2 * k, 0) for k in range(1, steps)]
    peers += [at(s, d) for s in (1, -1) for d in range(nx)]
    for peer in peers:
        pl.semaphore_signal(barrier, inc=1, device_id=peer, device_id_type=MESH)

    def prepare(layer):
        def one(u, carry):
            live = len_ref[u] - cache * events
            mask = lax.broadcasted_iota(jnp.int32, (events, LANES), 0) < live
            left = pltpu.roll(raws[layer][u, :, 0:LANES].astype(F32), DH, 1)
            right = raws[layer][u, :, LANES : 2 * LANES].astype(F32)
            hists[layer][u, 0] = jnp.where(mask, left, 0.0).astype(BF16)
            hists[layer][u, 1] = jnp.where(mask, right, 0.0).astype(BF16)
            return carry

        lax.fori_loop(0, users, one, 0)

    def gather(layer):
        def one(k, carry):
            for d in range(nx):
                to_x = (x + d) % nx
                block = hists[layer][req_ref[((z + 2 * k) % nz) * nx + to_x]]
                if d == 0:
                    stay[layer, x, k] = block
                else:
                    stay_s[layer, d - 1, k] = block
                for j in range(2):
                    to_z = (z + side * (1 - 2 * j) + 2 * k + nz) % nz
                    pair_s[layer, d, j, k] = hists[layer][req_ref[to_z * nx + to_x], j]
            return carry

        lax.fori_loop(0, steps, one, 0)

    def kv_send(layer, g):
        span = pl.ds(g, spans[layer])
        for d in range(nx):
            for j in range(2):
                remote(
                    pair_s.at[layer, d, j, span], pair.at[layer, x, j, span],
                    pair_ss.at[layer], pair_rs.at[layer, g], at(side * (1 - 2 * j), d),
                ).start()
            if d:
                remote(
                    stay_s.at[layer, d - 1, span], stay.at[layer, x, span],
                    stay_ss.at[layer], stay_rs.at[layer, g], at(0, d),
                ).start()

    def kv_wait(layer, g):
        span = pl.ds(g, spans[layer])
        drain(stay.at[layer, 0 : nx - 1, span], stay_rs.at[layer, g])
        drain(pair.at[layer, :, :, span], pair_rs.at[layer, g])

    loads[0].wait()
    prepare(0)
    gather(0)
    loads[1].wait()
    pl.semaphore_wait(barrier, len(peers))
    for d in range(1, nh):
        remote(tok.at[head], tok.at[head], tok_sem.at[0], tok_sem.at[1], h_peer(d)).start()
    for g in groups[0]:
        kv_send(0, g)
    loads[2].wait()
    prepare(1)
    gather(1)
    loads[3].wait()
    loads[4].wait()
    wo0[head] = wo_own[0]
    for b in range(nh):
        wo1_s[b // CORES, b % CORES] = wo_own[1, :, b * LANES : (b + 1) * LANES]
    wo1[head] = wo1_s[chip]
    drain(tok.at[0 : nh - 1], tok_sem.at[1])

    def project(layer, hidden, at_rows):
        count = hidden.shape[0]
        left = silu(dot(hidden, w_in[layer, :, 0:LANES]))
        right = pltpu.roll(silu(dot(hidden, w_in[layer, :, LANES : 2 * LANES])), DH, 1)
        low = lane_halves(count)
        q = (jnp.where(low, right, left).astype(BF16).astype(F32) * (0.5 * DH**-0.5)).astype(BF16)
        gates = jnp.where(low, left, right).astype(BF16)
        q_all[layer, 0, at_rows] = q
        return gates

    def send_projected(layer):
        for k in range(1, steps):
            remote(
                q_all.at[layer, 0], q_all.at[layer, steps - k], q_ss.at[layer], q_rs.at[layer, steps - k], at(2 * k, 0)
            ).start()
        gate_all[layer, head] = gate_s[layer, core]
        for d in range(1, nh):
            remote(
                gate_s.at[layer, (head + d) % CORES], gate_all.at[layer, head], g_ss.at[layer], g_rs.at[layer], h_peer(d)
            ).start()

    def attend(layer, k):
        q = q_all[layer, k]
        low = lane_halves(rows)
        zero = jnp.zeros_like(q)
        outs = []
        for j, q_one in ((0, jnp.where(low, zero, q)), (1, jnp.where(low, q, zero))):
            total = None
            for s in range(0, nx, 2):
                for keys in (stay[layer, s : s + 2, k, j], pair[layer, s : s + 2, j, k]):
                    kv = keys.reshape(2 * events, LANES)
                    t = dot(q_one, kv, ((1,), (1,)))
                    o = dot((t + t * jnp.tanh(t)).astype(BF16), kv)
                    total = o if total is None else total + o
            outs.append(total)
        block = jnp.where(low, outs[0], outs[1])
        centres = centre(block)
        centred = block - spread(centres)
        wide = centres.astype(F32)
        return centred, jnp.concatenate([wide[:, 0:half], wide[:, half:]], axis=0)

    def attention(layer):
        if 0 in groups[layer]:
            kv_wait(layer, 0)
        block, centres = attend(layer, 0)

        def one(k, carry):
            drain(q_all.at[layer, k], q_rs.at[layer, k])
            part, middle = attend(layer, k)
            part_s[layer, k - 1, 0:rows] = part.astype(BF16)
            part_s[layer, k - 1, rows : rows + EXTRA] = middle.astype(BF16)
            remote(
                part_s.at[layer, k - 1], part_r.at[layer, k - 1], p_ss.at[layer], p_rs.at[layer], at(2 * k, 0)
            ).start()
            return carry

        if layer == 0:
            for k in range(1, steps):
                kv_wait(layer, k)
                if k == steps - 1:
                    for g in groups[1]:
                        kv_send(1, g)
                one(k, 0)
            if steps == 1:
                for g in groups[1]:
                    kv_send(1, g)
        else:
            for k in range(1, steps):
                if k in groups[layer]:
                    kv_wait(layer, k)
                one(k, 0)
        if steps > 1:
            drain(part_r.at[layer], p_rs.at[layer])
        for k in range(steps - 1):
            block = block + part_r[layer, k, 0:rows].astype(F32)
            centres = centres + part_r[layer, k, rows : rows + EXTRA].astype(F32)
        for c in range(CORES):
            middle = centres[8 * c : 8 * c + 8]
            high = middle.astype(BF16).astype(F32)
            att_s[layer, c, 0:half] = block[c * half : (c + 1) * half].astype(BF16)
            att_s[layer, c, half : half + EXTRA] = jnp.concatenate([high, middle - high], axis=0).astype(BF16)
        for d in range(1, nh):
            remote(
                att_s.at[layer, (head + d) % CORES], att_all.at[layer, head], a_ss.at[layer], a_rs.at[layer], h_peer(d)
            ).start()
        att_all[layer, head] = att_s[layer, core]

    def normed(layer):
        total = jnp.zeros((half, LANES), F32)
        squares = jnp.zeros((half, LANES), F32)
        drain(gate_all.at[layer, 0 : nh - 1], g_rs.at[layer])
        drain(att_all.at[layer, 0 : nh - 1], a_rs.at[layer])
        for b in range(nh):
            block = att_all[layer, b, 0:half].astype(F32) + spread(att_all[layer, b, half : half + EXTRA])
            hid_f[b] = block
            total = total + block
            squares = squares + block * block
        width = nh * LANES
        mean = jnp.sum(total, axis=1, keepdims=True) * (1.0 / width)
        var = jnp.sum(squares, axis=1, keepdims=True) * (1.0 / width) - mean * mean
        scale = lax.rsqrt(var + 1e-05)
        return jnp.concatenate(
            [((hid_f[b] - mean) * scale * gate_all[layer, b].astype(F32)).astype(BF16) for b in range(nh)], axis=1
        )

    gates = project(0, jnp.concatenate([tok[b] for b in range(nh)], axis=1), pl.ds(0, rows))
    for c in range(CORES):
        gate_s[0, c] = gates[c * half : (c + 1) * half]
    send_projected(0)
    for d in range(1, nh // CORES):
        remote(wo0.at[head], wo0.at[head], wo_sem.at[0], wo_sem.at[1], h_peer(CORES * d)).start()
    remote(wo0.at[head], wo0.at[head], wo_sem.at[0], wo_sem.at[2], sibling).start()
    for d in range(1, nh):
        remote(wo1_s.at[((head + d) % nh) // CORES], wo1.at[head], wt_sem.at[0], wt_sem.at[1], h_peer(d)).start()
    attention(0)
    if nh > CORES:
        drain(wo0.at[0 : nh // CORES - 1], wo_sem.at[1])
    for d in range(1, nh // CORES):
        src = (head + CORES * d) % nh
        remote(wo0.at[src], wo0.at[src], wo_sem.at[0], wo_sem.at[2], sibling).start()
    drain(wo0.at[0 : nh // CORES], wo_sem.at[2])
    gated = normed(0)
    full = wo0[...].reshape(nh * LANES, nh * LANES)
    for b in range(0, nh, 2):
        branch = dot(gated, full[:, b * LANES : (b + 2) * LANES])
        for e in range(2):
            hid[core, b + e] = (
                tok[b + e, own_rows].astype(F32) + branch[:, e * LANES : (e + 1) * LANES]
            ).astype(BF16)
        remote(hid.at[core, b : b + 2], hid.at[core, b : b + 2], hid_sem.at[0], hid_sem.at[1], sibling).start()
    gate_s[1, core] = project(1, jnp.concatenate([hid[core, b] for b in range(nh)], axis=1), own_rows)
    drain(hid.at[0], hid_sem.at[1])
    gate_s[1, 1 - core] = project(1, jnp.concatenate([hid[1 - core, b] for b in range(nh)], axis=1), other_rows)
    send_projected(1)
    attention(1)
    drain(wo1.at[0 : nh - 1], wt_sem.at[1])
    gated = normed(1)

    def final(c):
        branch = dot(gated, wo1[:, c].reshape(nh * LANES, LANES))
        return (hid[core, chip * CORES + c].astype(F32) + branch).astype(BF16)

    last_s[...] = final(1 - core)
    remote(last_s, last_r, last_sem.at[0], last_sem.at[1], sibling).start()
    out_ref[own_rows] = final(core)

    drain(tok.at[0 : nh - 1], tok_sem.at[0])
    drain(wo0.at[0 : nh - 1], wo_sem.at[0])
    drain(wo1.at[0 : nh - 1], wt_sem.at[0])
    drain(hid.at[0], hid_sem.at[0])
    for layer in range(LAYERS):
        drain(stay_s.at[layer], stay_ss.at[layer])
        drain(pair_s.at[layer], pair_ss.at[layer])
        if steps > 1:
            drain(q_all.at[layer, 0 : steps - 1], q_ss.at[layer])
            drain(part_s.at[layer], p_ss.at[layer])
        drain(gate_all.at[layer, 0 : nh - 1], g_ss.at[layer])
        drain(att_all.at[layer, 0 : nh - 1], a_ss.at[layer])
    drain(last_r, last_sem.at[1])
    drain(last_s, last_sem.at[0])
    out_ref[other_rows] = last_r[...]


def body(x_size, nc, nh, tokens, request_user, hist_len, history, w_in, w_out):
    nx = x_size
    nz = nc // nx
    steps = nz // 2
    rows = tokens.shape[0]
    half = rows // CORES
    users, events = history.shape[1], history.shape[2]
    width = nh * LANES
    hbm = pl.BlockSpec(memory_space=pltpu.HBM)
    smem = pl.BlockSpec(memory_space=pltpu.SMEM)
    sem = pltpu.SemaphoreType.DMA
    vmem = pltpu.VMEM
    return pl.pallas_call(
        functools.partial(kernel, (nz, nx, nh)),
        out_shape=jax.ShapeDtypeStruct((rows, LANES), BF16),
        in_specs=[smem, smem, hbm, hbm, hbm, hbm],
        out_specs=pl.BlockSpec(memory_space=pltpu.VMEM),
        scratch_shapes=[
            vmem((users, events, 2 * LANES), BF16),
            vmem((users, events, 2 * LANES), BF16),
            vmem((users, 2, events, LANES), BF16),
            vmem((users, 2, events, LANES), BF16),
            vmem((LAYERS, nx - 1, steps, 2, events, LANES), BF16),
            vmem((LAYERS, nx, steps, 2, events, LANES), BF16),
            vmem((LAYERS, nx, 2, steps, events, LANES), BF16),
            vmem((LAYERS, nx, 2, steps, events, LANES), BF16),
            vmem((nh, rows, LANES), BF16),
            vmem((CORES, nh, half, LANES), BF16),
            vmem((nh, half, LANES), F32),
            vmem((LAYERS, width, 2 * LANES), BF16),
            vmem((nh, LANES, width), BF16),
            vmem((LAYERS, LANES, width), BF16),
            vmem((nh // CORES, CORES, LANES, LANES), BF16),
            vmem((nh, CORES, LANES, LANES), BF16),
            vmem((LAYERS, steps, rows, LANES), BF16),
            vmem((LAYERS, CORES, half, LANES), BF16),
            vmem((LAYERS, nh, half, LANES), BF16),
            vmem((LAYERS, max(steps - 1, 1), rows + EXTRA, LANES), BF16),
            vmem((LAYERS, max(steps - 1, 1), rows + EXTRA, LANES), BF16),
            vmem((LAYERS, CORES, half + EXTRA, LANES), BF16),
            vmem((LAYERS, nh, half + EXTRA, LANES), BF16),
            vmem((half, LANES), BF16),
            vmem((half, LANES), BF16),
            sem((5,)),
            sem((2,)),
            sem((LAYERS,)), sem((LAYERS, steps)),
            sem((LAYERS,)), sem((LAYERS, steps)),
            sem((LAYERS,)), sem((LAYERS, steps)),
            sem((LAYERS,)), sem((LAYERS,)),
            sem((LAYERS,)), sem((LAYERS,)),
            sem((LAYERS,)), sem((LAYERS,)),
            sem((3,)), sem((2,)), sem((2,)), sem((2,)),
        ],
        compiler_params=pltpu.CompilerParams(
            collective_id=0, has_side_effects=True, vmem_limit_bytes=60 * 1024 * 1024
        ),
    )(request_user.reshape(-1), hist_len, tokens, history, w_in, w_out)


def solution(mesh):
    in_specs = (
        P("cache", "head"),
        P(),
        P(),
        P(None, None, "cache", "head"),
        P(None, None, "head"),
        P(None, "head", None),
    )
    run = functools.partial(body, X_SIZE, mesh.shape["cache"], mesh.shape["head"])
    return jax.shard_map(run, mesh=mesh, in_specs=in_specs, out_specs=P("cache", "head"), check_vma=False)
```

```python
import functools

import jax
import jax.numpy as jnp
from jax import lax
from jax.experimental import pallas as pl
from jax.experimental.pallas import tpu as pltpu
from jax.sharding import PartitionSpec as P

DH = 64
LAYERS = 2
LANES = 128
X_SIZE = 4
CORES = 2
EXTRA = 16
PACE = ((0, 1), (2, 3), (0, 1), (2,), (), (3,))
MESH = pl.DeviceIdType.MESH
F32 = jnp.float32
BF16 = jnp.bfloat16


def dot(a, b, dims=((1,), (0,))):
    return lax.dot_general(a, b, (dims, ((), ())), preferred_element_type=F32)


def silu(v):
    half = v * 0.5
    return half + half * jnp.tanh(half)


def lane_halves(rows):
    return lax.broadcasted_iota(jnp.int32, (rows, LANES), 1) < DH


def head_rows(value, dtype):
    row = lax.broadcasted_iota(jnp.int32, (8, LANES), 0)
    lane = lax.broadcasted_iota(jnp.int32, (8, LANES), 1)
    own = ((row == 0) & (lane < DH)) | ((row == 1) & (lane >= DH))
    return jnp.where(own, value, 0.0).astype(dtype)


def spread(flat):
    pick = head_rows(1.0, F32)
    if flat.shape[0] == 16:
        pick = jnp.concatenate([pick, pick], axis=0)
    return dot(flat, pick.astype(BF16), ((0,), (0,)))


def centre(block):
    return dot(head_rows(1.0 / DH, BF16), block.astype(BF16), ((1,), (1,))).astype(BF16)


def kernel(
    sizes, req_ref, len_ref, tok_hbm, hist_hbm, w_in_hbm, w_out_hbm, out_ref,
    raw0, raw1, hist0, hist1, stay_s, stay, pair_s, pair, tok, hid, hid_f, w_in, wo0, wo_own, wo1_s, wo1,
    q_all, gate_s, gate_all, part_s, part_r, att_s, att_all, last_s, last_r,
    load_sem, tok_sem, stay_ss, stay_rs, pair_ss, pair_rs, q_ss, q_rs, p_ss, p_rs, g_ss, g_rs, a_ss, a_rs, wo_sem, wt_sem,
    hid_sem, last_sem,
):
    nz, nx, nh = sizes
    steps = nz // 2
    users, events = raw0.shape[0], raw0.shape[1]
    rows = tok.shape[1]
    half = rows // CORES
    raws, hists = (raw0, raw1), (hist0, hist1)
    cache, head = lax.axis_index("cache"), lax.axis_index("head")
    z, x = cache // nx, cache % nx
    chip, core = head // CORES, head % CORES
    own_rows = pl.ds(pl.multiple_of(core * half, half), half)
    other_rows = pl.ds(pl.multiple_of((1 - core) * half, half), half)
    side = 1 - 2 * (z % 2)

    def at(d_z, d_x):
        return (((z + d_z + nz) % nz) * nx + (x + d_x) % nx, head)

    def h_peer(d):
        return (cache, (head + d) % nh)

    sibling = (cache, head + 1 - 2 * core)

    def remote(src, dst, send, recv, device):
        return pltpu.make_async_remote_copy(
            src_ref=src, dst_ref=dst, send_sem=send, recv_sem=recv, device_id=device, device_id_type=MESH
        )

    def drain(ref, sem):
        pltpu.make_async_copy(ref, ref, sem).wait()

    loads = [
        pltpu.make_async_copy(hist_hbm.at[0], raw0, load_sem.at[0]),
        pltpu.make_async_copy(tok_hbm, tok.at[head], load_sem.at[1]),
        pltpu.make_async_copy(hist_hbm.at[1], raw1, load_sem.at[2]),
        pltpu.make_async_copy(w_in_hbm, w_in, load_sem.at[3]),
        pltpu.make_async_copy(w_out_hbm, wo_own, load_sem.at[4]),
    ]
    for load in loads:
        load.start()

    barrier = pltpu.get_barrier_semaphore()
    peers = [at(0, d) for d in range(1, nx)] + [h_peer(d) for d in range(1, nh)]
    peers += [at(2 * k, 0) for k in range(1, steps)]
    peers += [at(s, d) for s in (1, -1) for d in range(nx)]
    for peer in peers:
        pl.semaphore_signal(barrier, inc=1, device_id=peer, device_id_type=MESH)

    def prepare(layer):
        def one(u, carry):
            live = len_ref[u] - cache * events
            mask = lax.broadcasted_iota(jnp.int32, (events, LANES), 0) < live
            left = pltpu.roll(raws[layer][u, :, 0:LANES].astype(F32), DH, 1)
            right = raws[layer][u, :, LANES : 2 * LANES].astype(F32)
            hists[layer][u, 0] = jnp.where(mask, left, 0.0).astype(BF16)
            hists[layer][u, 1] = jnp.where(mask, right, 0.0).astype(BF16)
            return carry

        lax.fori_loop(0, users, one, 0)

    def gather(layer):
        def one(k, carry):
            for d in range(nx):
                to_x = (x + d) % nx
                block = hists[layer][req_ref[((z + 2 * k) % nz) * nx + to_x]]
                if d == 0:
                    stay[layer, x, k] = block
                else:
                    stay_s[layer, d - 1, k] = block
                for j in range(2):
                    to_z = (z + side * (1 - 2 * j) + 2 * k + nz) % nz
                    pair_s[layer, d, j, k] = hists[layer][req_ref[to_z * nx + to_x], j]
            return carry

        lax.fori_loop(0, steps, one, 0)

    def kv_send(layer, g):
        span = pl.ds(g, 1)
        for d in range(nx):
            for j in range(2):
                remote(
                    pair_s.at[layer, d, j, span], pair.at[layer, x, j, span],
                    pair_ss.at[layer], pair_rs.at[layer, g], at(side * (1 - 2 * j), d),
                ).start()
            if d:
                remote(
                    stay_s.at[layer, d - 1, span], stay.at[layer, x, span],
                    stay_ss.at[layer], stay_rs.at[layer, g], at(0, d),
                ).start()

    def kv_batch(layer, batch):
        for g in batch:
            if g < steps:
                kv_send(layer, g)

    def kv_wait(layer, g):
        span = pl.ds(g, 1)
        drain(stay.at[layer, 0 : nx - 1, span], stay_rs.at[layer, g])
        drain(pair.at[layer, :, :, span], pair_rs.at[layer, g])

    loads[0].wait()
    prepare(0)
    gather(0)
    loads[1].wait()
    pl.semaphore_wait(barrier, len(peers))
    for d in range(1, nh):
        remote(tok.at[head], tok.at[head], tok_sem.at[0], tok_sem.at[1], h_peer(d)).start()
    kv_batch(0, PACE[0])
    loads[2].wait()
    prepare(1)
    gather(1)
    loads[3].wait()
    loads[4].wait()
    wo0[head] = wo_own[0]
    for b in range(nh):
        wo1_s[b // CORES, b % CORES] = wo_own[1, :, b * LANES : (b + 1) * LANES]
    wo1[head] = wo1_s[chip]
    drain(tok.at[0 : nh - 1], tok_sem.at[1])

    def project(layer, hidden, at_rows):
        count = hidden.shape[0]
        left = silu(dot(hidden, w_in[layer, :, 0:LANES]))
        right = pltpu.roll(silu(dot(hidden, w_in[layer, :, LANES : 2 * LANES])), DH, 1)
        low = lane_halves(count)
        q = (jnp.where(low, right, left).astype(BF16).astype(F32) * (0.5 * DH**-0.5)).astype(BF16)
        gates = jnp.where(low, left, right).astype(BF16)
        q_all[layer, 0, at_rows] = q
        return gates

    def send_projected(layer):
        for k in range(1, steps):
            remote(
                q_all.at[layer, 0], q_all.at[layer, steps - k], q_ss.at[layer], q_rs.at[layer, steps - k], at(2 * k, 0)
            ).start()
        gate_all[layer, head] = gate_s[layer, core]
        for d in range(1, nh):
            remote(
                gate_s.at[layer, (head + d) % CORES], gate_all.at[layer, head], g_ss.at[layer], g_rs.at[layer], h_peer(d)
            ).start()

    def attend(layer, k):
        q = q_all[layer, k]
        low = lane_halves(rows)
        zero = jnp.zeros_like(q)
        outs = []
        for j, q_one in ((0, jnp.where(low, zero, q)), (1, jnp.where(low, q, zero))):
            total = None
            for s in range(0, nx, 2):
                for keys in (stay[layer, s : s + 2, k, j], pair[layer, s : s + 2, j, k]):
                    kv = keys.reshape(2 * events, LANES)
                    t = dot(q_one, kv, ((1,), (1,)))
                    o = dot((t + t * jnp.tanh(t)).astype(BF16), kv)
                    total = o if total is None else total + o
            outs.append(total)
        block = jnp.where(low, outs[0], outs[1])
        centres = centre(block)
        centred = block - spread(centres)
        wide = centres.astype(F32)
        return centred, jnp.concatenate([wide[:, 0:half], wide[:, half:]], axis=0)

    def attention(layer):
        kv_wait(layer, 0)
        block, centres = attend(layer, 0)

        def one(k, carry):
            drain(q_all.at[layer, k], q_rs.at[layer, k])
            part, middle = attend(layer, k)
            part_s[layer, k - 1, 0:rows] = part.astype(BF16)
            part_s[layer, k - 1, rows : rows + EXTRA] = middle.astype(BF16)
            remote(
                part_s.at[layer, k - 1], part_r.at[layer, k - 1], p_ss.at[layer], p_rs.at[layer], at(2 * k, 0)
            ).start()
            return carry

        for k in range(1, steps):
            kv_wait(layer, k)
            one(k, 0)
        if layer == 0:
            kv_batch(1, PACE[2])
        if steps > 1:
            drain(part_r.at[layer], p_rs.at[layer])
        for k in range(steps - 1):
            block = block + part_r[layer, k, 0:rows].astype(F32)
            centres = centres + part_r[layer, k, rows : rows + EXTRA].astype(F32)
        for c in range(CORES):
            middle = centres[8 * c : 8 * c + 8]
            high = middle.astype(BF16).astype(F32)
            att_s[layer, c, 0:half] = block[c * half : (c + 1) * half].astype(BF16)
            att_s[layer, c, half : half + EXTRA] = jnp.concatenate([high, middle - high], axis=0).astype(BF16)
        for d in range(1, nh):
            remote(
                att_s.at[layer, (head + d) % CORES], att_all.at[layer, head], a_ss.at[layer], a_rs.at[layer], h_peer(d)
            ).start()
        att_all[layer, head] = att_s[layer, core]
        if layer == 0:
            kv_batch(1, PACE[3])

    def normed(layer):
        total = jnp.zeros((half, LANES), F32)
        squares = jnp.zeros((half, LANES), F32)
        drain(gate_all.at[layer, 0 : nh - 1], g_rs.at[layer])
        drain(att_all.at[layer, 0 : nh - 1], a_rs.at[layer])
        for b in range(nh):
            block = att_all[layer, b, 0:half].astype(F32) + spread(att_all[layer, b, half : half + EXTRA])
            hid_f[b] = block
            total = total + block
            squares = squares + block * block
        width = nh * LANES
        mean = jnp.sum(total, axis=1, keepdims=True) * (1.0 / width)
        var = jnp.sum(squares, axis=1, keepdims=True) * (1.0 / width) - mean * mean
        scale = lax.rsqrt(var + 1e-05)
        return jnp.concatenate(
            [((hid_f[b] - mean) * scale * gate_all[layer, b].astype(F32)).astype(BF16) for b in range(nh)], axis=1
        )

    gates = project(0, jnp.concatenate([tok[b] for b in range(nh)], axis=1), pl.ds(0, rows))
    for c in range(CORES):
        gate_s[0, c] = gates[c * half : (c + 1) * half]
    send_projected(0)
    kv_batch(0, PACE[1])
    for d in range(1, nh // CORES):
        remote(wo0.at[head], wo0.at[head], wo_sem.at[0], wo_sem.at[1], h_peer(CORES * d)).start()
    remote(wo0.at[head], wo0.at[head], wo_sem.at[0], wo_sem.at[2], sibling).start()
    for d in range(1, nh):
        remote(wo1_s.at[((head + d) % nh) // CORES], wo1.at[head], wt_sem.at[0], wt_sem.at[1], h_peer(d)).start()
    attention(0)
    if nh > CORES:
        drain(wo0.at[0 : nh // CORES - 1], wo_sem.at[1])
    for d in range(1, nh // CORES):
        src = (head + CORES * d) % nh
        remote(wo0.at[src], wo0.at[src], wo_sem.at[0], wo_sem.at[2], sibling).start()
    drain(wo0.at[0 : nh // CORES], wo_sem.at[2])
    gated = normed(0)
    kv_batch(1, PACE[4])
    full = wo0[...].reshape(nh * LANES, nh * LANES)
    for b in range(0, nh, 2):
        branch = dot(gated, full[:, b * LANES : (b + 2) * LANES])
        for e in range(2):
            hid[core, b + e] = (
                tok[b + e, own_rows].astype(F32) + branch[:, e * LANES : (e + 1) * LANES]
            ).astype(BF16)
        remote(hid.at[core, b : b + 2], hid.at[core, b : b + 2], hid_sem.at[0], hid_sem.at[1], sibling).start()
    gate_s[1, core] = project(1, jnp.concatenate([hid[core, b] for b in range(nh)], axis=1), own_rows)
    drain(hid.at[0], hid_sem.at[1])
    gate_s[1, 1 - core] = project(1, jnp.concatenate([hid[1 - core, b] for b in range(nh)], axis=1), other_rows)
    send_projected(1)
    kv_batch(1, PACE[5])
    attention(1)
    drain(wo1.at[0 : nh - 1], wt_sem.at[1])
    gated = normed(1)

    def final(c):
        branch = dot(gated, wo1[:, c].reshape(nh * LANES, LANES))
        return (hid[core, chip * CORES + c].astype(F32) + branch).astype(BF16)

    last_s[...] = final(1 - core)
    remote(last_s, last_r, last_sem.at[0], last_sem.at[1], sibling).start()
    out_ref[own_rows] = final(core)

    drain(tok.at[0 : nh - 1], tok_sem.at[0])
    drain(wo0.at[0 : nh - 1], wo_sem.at[0])
    drain(wo1.at[0 : nh - 1], wt_sem.at[0])
    drain(hid.at[0], hid_sem.at[0])
    for layer in range(LAYERS):
        drain(stay_s.at[layer], stay_ss.at[layer])
        drain(pair_s.at[layer], pair_ss.at[layer])
        if steps > 1:
            drain(q_all.at[layer, 0 : steps - 1], q_ss.at[layer])
            drain(part_s.at[layer], p_ss.at[layer])
        drain(gate_all.at[layer, 0 : nh - 1], g_ss.at[layer])
        drain(att_all.at[layer, 0 : nh - 1], a_ss.at[layer])
    drain(last_r, last_sem.at[1])
    drain(last_s, last_sem.at[0])
    out_ref[other_rows] = last_r[...]


def body(x_size, nc, nh, tokens, request_user, hist_len, history, w_in, w_out):
    nx = x_size
    nz = nc // nx
    steps = nz // 2
    rows = tokens.shape[0]
    half = rows // CORES
    users, events = history.shape[1], history.shape[2]
    width = nh * LANES
    hbm = pl.BlockSpec(memory_space=pltpu.HBM)
    smem = pl.BlockSpec(memory_space=pltpu.SMEM)
    sem = pltpu.SemaphoreType.DMA
    vmem = pltpu.VMEM
    return pl.pallas_call(
        functools.partial(kernel, (nz, nx, nh)),
        out_shape=jax.ShapeDtypeStruct((rows, LANES), BF16),
        in_specs=[smem, smem, hbm, hbm, hbm, hbm],
        out_specs=pl.BlockSpec(memory_space=pltpu.VMEM),
        scratch_shapes=[
            vmem((users, events, 2 * LANES), BF16),
            vmem((users, events, 2 * LANES), BF16),
            vmem((users, 2, events, LANES), BF16),
            vmem((users, 2, events, LANES), BF16),
            vmem((LAYERS, nx - 1, steps, 2, events, LANES), BF16),
            vmem((LAYERS, nx, steps, 2, events, LANES), BF16),
            vmem((LAYERS, nx, 2, steps, events, LANES), BF16),
            vmem((LAYERS, nx, 2, steps, events, LANES), BF16),
            vmem((nh, rows, LANES), BF16),
            vmem((CORES, nh, half, LANES), BF16),
            vmem((nh, half, LANES), F32),
            vmem((LAYERS, width, 2 * LANES), BF16),
            vmem((nh, LANES, width), BF16),
            vmem((LAYERS, LANES, width), BF16),
            vmem((nh // CORES, CORES, LANES, LANES), BF16),
            vmem((nh, CORES, LANES, LANES), BF16),
            vmem((LAYERS, steps, rows, LANES), BF16),
            vmem((LAYERS, CORES, half, LANES), BF16),
            vmem((LAYERS, nh, half, LANES), BF16),
            vmem((LAYERS, max(steps - 1, 1), rows + EXTRA, LANES), BF16),
            vmem((LAYERS, max(steps - 1, 1), rows + EXTRA, LANES), BF16),
            vmem((LAYERS, CORES, half + EXTRA, LANES), BF16),
            vmem((LAYERS, nh, half + EXTRA, LANES), BF16),
            vmem((half, LANES), BF16),
            vmem((half, LANES), BF16),
            sem((5,)),
            sem((2,)),
            sem((LAYERS,)), sem((LAYERS, steps)),
            sem((LAYERS,)), sem((LAYERS, steps)),
            sem((LAYERS,)), sem((LAYERS, steps)),
            sem((LAYERS,)), sem((LAYERS,)),
            sem((LAYERS,)), sem((LAYERS,)),
            sem((LAYERS,)), sem((LAYERS,)),
            sem((3,)), sem((2,)), sem((2,)), sem((2,)),
        ],
        compiler_params=pltpu.CompilerParams(
            collective_id=0, has_side_effects=True, vmem_limit_bytes=60 * 1024 * 1024
        ),
    )(request_user.reshape(-1), hist_len, tokens, history, w_in, w_out)


def solution(mesh):
    in_specs = (
        P("cache", "head"),
        P(),
        P(),
        P(None, None, "cache", "head"),
        P(None, None, "head"),
        P(None, "head", None),
    )
    run = functools.partial(body, X_SIZE, mesh.shape["cache"], mesh.shape["head"])
    return jax.shard_map(run, mesh=mesh, in_specs=in_specs, out_specs=P("cache", "head"), check_vma=False)
```

```python
import functools

import jax
import jax.numpy as jnp
from jax import lax
from jax.experimental import pallas as pl
from jax.experimental.pallas import tpu as pltpu
from jax.sharding import PartitionSpec as P

DH = 64
LAYERS = 2
LANES = 128
X_SIZE = 4
CORES = 2
PARTS = 2
FIRST = (2, 1, 3)
ORDER = (((2, -1), (1, -1), (3, -1), (0, -1)), ((0, -1), (2, -1), (1, -1), (3, -1)))
EXTRA = 16
OWN, NEAR = True, False
PACE = (
    ((0, OWN, (2, 1, 3, 0)), (0, NEAR, (2, 1, 3, 0))), (),
    ((1, NEAR, (0, 2, 1, 3)), (1, OWN, (0, 2, 1, 3))), (), (), (),
)
MESH = pl.DeviceIdType.MESH
F32 = jnp.float32
BF16 = jnp.bfloat16


def dot(a, b, dims=((1,), (0,))):
    return lax.dot_general(a, b, (dims, ((), ())), preferred_element_type=F32)


def silu(v):
    half = v * 0.5
    return half + half * jnp.tanh(half)


def lane_halves(rows):
    return lax.broadcasted_iota(jnp.int32, (rows, LANES), 1) < DH


def head_rows(value, dtype):
    row = lax.broadcasted_iota(jnp.int32, (8, LANES), 0)
    lane = lax.broadcasted_iota(jnp.int32, (8, LANES), 1)
    own = ((row == 0) & (lane < DH)) | ((row == 1) & (lane >= DH))
    return jnp.where(own, value, 0.0).astype(dtype)


def spread(flat):
    pick = head_rows(1.0, F32)
    if flat.shape[0] == 16:
        pick = jnp.concatenate([pick, pick], axis=0)
    return dot(flat, pick.astype(BF16), ((0,), (0,)))


def centre(block):
    return dot(head_rows(1.0 / DH, BF16), block.astype(BF16), ((1,), (1,))).astype(BF16)


def kernel(
    sizes, req_ref, len_ref, tok_hbm, hist_hbm, w_in_hbm, w_out_hbm, out_ref,
    raw0, raw1, hist0, hist1, stay_s, stay, pair_s, pair, own_tok, hid0, hid, hid_f, w_in, wo0, wo_own, wo1_s, wo1,
    q_all, gate_s, gate_all, part_s, part_r, att_s, att_all, acc, mid, last_s, last_r,
    load_sem, tok_ss, tok_rs, fwd_ss, fwd_rs, stay_ss, stay_rs, pair_ss, pair_rs, q_ss, q_rs, p_ss, p_rs, g_ss, g_rs, a_ss, a_rs, wo_sem, wt_sem,
    hid_ss, hid_rs, last_sem,
):
    nz, nx, nh = sizes
    steps = nz // 2
    users, events = raw0.shape[0], raw0.shape[1]
    half = hid0.shape[3]
    rows = CORES * half
    raws, hists = (raw0, raw1), (hist0, hist1)
    cache, head = lax.axis_index("cache"), lax.axis_index("head")
    z, x = cache // nx, cache % nx
    chip, core = head // CORES, head % CORES
    side = 1 - 2 * (z % 2)

    def part_rows(p, c):
        return pl.ds(pl.multiple_of(p * rows + c * half, half), half)

    def at(d_z, d_x):
        return (((z + d_z + nz) % nz) * nx + (x + d_x) % nx, head)

    def h_peer(d):
        return (cache, (head + d) % nh)

    sibling = (cache, head + 1 - 2 * core)

    def remote(src, dst, send, recv, device):
        return pltpu.make_async_remote_copy(
            src_ref=src, dst_ref=dst, send_sem=send, recv_sem=recv, device_id=device, device_id_type=MESH
        )

    def drain(ref, sem):
        pltpu.make_async_copy(ref, ref, sem).wait()

    loads = [
        pltpu.make_async_copy(hist_hbm.at[0], raw0, load_sem.at[0]),
        pltpu.make_async_copy(tok_hbm, own_tok, load_sem.at[1]),
        pltpu.make_async_copy(hist_hbm.at[1], raw1, load_sem.at[2]),
        pltpu.make_async_copy(w_in_hbm, w_in, load_sem.at[3]),
        pltpu.make_async_copy(w_out_hbm, wo_own, load_sem.at[4]),
    ]
    for load in loads:
        load.start()

    barrier = pltpu.get_barrier_semaphore()
    peers = [at(0, d) for d in range(1, nx)] + [h_peer(d) for d in range(1, nh)]
    peers += [at(2 * k, 0) for k in range(1, steps)]
    peers += [at(s, d) for s in (1, -1) for d in range(nx)]
    for peer in peers:
        pl.semaphore_signal(barrier, inc=1, device_id=peer, device_id_type=MESH)

    def prepare(layer):
        def one(u, carry):
            live = len_ref[u] - cache * events
            mask = lax.broadcasted_iota(jnp.int32, (events, LANES), 0) < live
            left = pltpu.roll(raws[layer][u, :, 0:LANES].astype(F32), DH, 1)
            right = raws[layer][u, :, LANES : 2 * LANES].astype(F32)
            hists[layer][u, 0] = jnp.where(mask, left, 0.0).astype(BF16)
            hists[layer][u, 1] = jnp.where(mask, right, 0.0).astype(BF16)
            return carry

        lax.fori_loop(0, users, one, 0)

    def gather(layer):
        def one(k, carry):
            for d in range(nx):
                to_x = (x + d) % nx
                block = hists[layer][req_ref[((z + 2 * k) % nz) * nx + to_x]]
                if d == 0:
                    stay[layer, x, k] = block
                else:
                    stay_s[layer, d - 1, k] = block
                for j in range(2):
                    to_z = (z + side * (1 - 2 * j) + 2 * k + nz) % nz
                    pair_s[layer, d, j, k] = hists[layer][req_ref[to_z * nx + to_x], j]
            return carry

        lax.fori_loop(0, steps, one, 0)

    def kv_send(layer, own, g):
        span = pl.ds(g, 1)
        for d in range(nx):
            if own and d:
                remote(
                    stay_s.at[layer, d - 1, span], stay.at[layer, x, span],
                    stay_ss.at[layer], stay_rs.at[layer, g], at(0, d),
                ).start()
            for j in range(0 if own else 2):
                remote(
                    pair_s.at[layer, d, j, span], pair.at[layer, x, j, span],
                    pair_ss.at[layer], pair_rs.at[layer, g], at(side * (1 - 2 * j), d),
                ).start()

    def kv_point(point):
        for layer, own, batch in PACE[point]:
            for g in batch:
                if g < steps:
                    kv_send(layer, own, g)

    def kv_wait(layer, g):
        span = pl.ds(g, 1)
        drain(stay.at[layer, 0 : nx - 1, span], stay_rs.at[layer, g])
        drain(pair.at[layer, :, :, span], pair_rs.at[layer, g])

    loads[0].wait()
    prepare(0)
    gather(0)
    loads[1].wait()
    for p in range(PARTS):
        hid0[p, core, head] = own_tok[part_rows(p, core)]
    pl.semaphore_wait(barrier, len(peers))
    for p in range(PARTS):
        for d in range(1, nh):
            to = (head + d) % CORES
            remote(own_tok.at[part_rows(p, to)], hid0.at[p, to, head], tok_ss, tok_rs.at[p], h_peer(d)).start()
    loads[4].wait()
    wo0[head] = wo_own[0]
    for d in range(1, nh // CORES):
        remote(wo0.at[head], wo0.at[head], wo_sem.at[0], wo_sem.at[1], h_peer(CORES * d)).start()
    remote(wo0.at[head], wo0.at[head], wo_sem.at[0], wo_sem.at[2], sibling).start()
    kv_point(0)
    loads[2].wait()
    prepare(1)
    gather(1)
    loads[3].wait()
    for b in range(nh):
        wo1_s[b // CORES, b % CORES] = wo_own[1, :, b * LANES : (b + 1) * LANES]
    wo1[head] = wo1_s[chip]

    def project(layer, p, halves):
        hidden = jnp.concatenate([halves[p, :, b].reshape(rows, LANES) for b in range(nh)], axis=1)
        left = silu(dot(hidden, w_in[layer, :, 0:LANES]))
        right = pltpu.roll(silu(dot(hidden, w_in[layer, :, LANES : 2 * LANES])), DH, 1)
        low = lane_halves(rows)
        q = (jnp.where(low, right, left).astype(BF16).astype(F32) * (0.5 * DH**-0.5)).astype(BF16)
        gates = jnp.where(low, left, right).astype(BF16)
        q_all[layer, p, 0] = q
        for c in range(CORES):
            gate_s[layer, p, c] = gates[c * half : (c + 1) * half]
        for k in [k for k in FIRST if k < steps]:
            remote(
                q_all.at[layer, p, 0], q_all.at[layer, p, steps - k],
                q_ss.at[layer], q_rs.at[layer, p, steps - k], at(2 * k, 0),
            ).start()

    def send_gates(layer):
        for p in range(PARTS):
            gate_all[layer, p, head] = gate_s[layer, p, core]
            for d in range(1, nh):
                remote(
                    gate_s.at[layer, p, (head + d) % CORES], gate_all.at[layer, p, head],
                    g_ss.at[layer], g_rs.at[layer, p], h_peer(d),
                ).start()

    def attend(layer, k, q):
        low = lane_halves(q.shape[0])
        zero = jnp.zeros_like(q)
        outs = []
        for j, q_one in ((0, jnp.where(low, zero, q)), (1, jnp.where(low, q, zero))):
            kvs, weights = [], []
            for s in range(0, nx, 2):
                for keys in (stay[layer, s : s + 2, k, j], pair[layer, s : s + 2, j, k]):
                    kv = keys.reshape(2 * events, LANES)
                    t = dot(q_one, kv, ((1,), (1,)))
                    kvs.append(kv)
                    weights.append((t + t * jnp.tanh(t)).astype(BF16))
            outs.append(dot(jnp.concatenate(weights, axis=1), jnp.concatenate(kvs, axis=0)))
        block = jnp.where(low, outs[0], outs[1])
        centres = centre(block)
        return block - spread(centres), centres.astype(F32)

    def give(layer, k, p, block, centres):
        part_s[layer, p, k - 1, 0:rows] = block.astype(BF16)
        part_s[layer, p, k - 1, rows : rows + EXTRA] = jnp.concatenate(
            [centres, jnp.zeros_like(centres)], axis=0
        ).astype(BF16)
        remote(
            part_s.at[layer, p, k - 1], part_r.at[layer, p, k - 1], p_ss.at[layer], p_rs.at[layer, p], at(2 * k, 0)
        ).start()

    def both(layer, k):
        q = jnp.concatenate([q_all[layer, p, k] for p in range(PARTS)], axis=0)
        block, centres = attend(layer, k, q)
        return [(block[p * rows : (p + 1) * rows], centres[:, p * rows : (p + 1) * rows]) for p in range(PARTS)]

    def attention(layer):
        def own():
            kv_wait(layer, 0)
            for p, (block, centres) in enumerate(both(layer, 0)):
                acc[p] = block
                mid[p] = centres

        waited = [0]
        for k, p in ORDER[layer]:
            if k == 0:
                if layer == 0:
                    kv_point(2)
                own()
            elif k < steps:
                if k not in waited:
                    kv_wait(layer, k)
                    waited.append(k)
                for e in range(PARTS) if p < 0 else (p,):
                    drain(q_all.at[layer, e, k], q_rs.at[layer, e, k])
                if p < 0:
                    for e, (block, centres) in enumerate(both(layer, k)):
                        give(layer, k, e, block, centres)
                else:
                    give(layer, k, p, *attend(layer, k, q_all[layer, p, k]))

    def send_attended(layer):
        for p in range(PARTS):
            block, centres = acc[p], mid[p]
            if steps > 1:
                drain(part_r.at[layer, p], p_rs.at[layer, p])
            for k in range(steps - 1):
                block = block + part_r[layer, p, k, 0:rows].astype(F32)
                centres = centres + part_r[layer, p, k, rows : rows + EXTRA].astype(F32)[0:8]
            high = centres.astype(BF16).astype(F32)
            pairs = jnp.concatenate([high, centres - high], axis=0)
            for c in range(CORES):
                att_s[layer, p, c, 0:half] = block[c * half : (c + 1) * half].astype(BF16)
                shifted = pairs if c == 0 else pltpu.roll(pairs, rows - c * half, 1)
                att_s[layer, p, c, half : half + EXTRA] = shifted.astype(BF16)
            for d in range(1, nh):
                remote(
                    att_s.at[layer, p, (head + d) % CORES], att_all.at[layer, p, head],
                    a_ss.at[layer], a_rs.at[layer, p], h_peer(d),
                ).start()
            att_all[layer, p, head] = att_s[layer, p, core]

    def normed(layer, p):
        total = jnp.zeros((half, LANES), F32)
        squares = jnp.zeros((half, LANES), F32)
        drain(gate_all.at[layer, p, 0 : nh - 1], g_rs.at[layer, p])
        drain(att_all.at[layer, p, 0 : nh - 1], a_rs.at[layer, p])
        for b in range(nh):
            block = att_all[layer, p, b, 0:half].astype(F32) + spread(
                att_all[layer, p, b, half : half + EXTRA][:, 0:half]
            )
            hid_f[b] = block
            total = total + block
            squares = squares + block * block
        width = nh * LANES
        mean = jnp.sum(total, axis=1, keepdims=True) * (1.0 / width)
        var = jnp.sum(squares, axis=1, keepdims=True) * (1.0 / width) - mean * mean
        scale = lax.rsqrt(var + 1e-05)
        return jnp.concatenate(
            [((hid_f[b] - mean) * scale * gate_all[layer, p, b].astype(F32)).astype(BF16) for b in range(nh)], axis=1
        )

    for p in range(PARTS):
        drain(hid0.at[p, 0, 0 : nh - 1], tok_rs.at[p])
        remote(hid0.at[p, core], hid0.at[p, core], fwd_ss, fwd_rs.at[p], sibling).start()
    for p in range(PARTS):
        drain(hid0.at[p, 0], fwd_rs.at[p])
        project(0, p, hid0)
    kv_point(1)
    send_gates(0)
    attention(0)
    if nh > CORES:
        drain(wo0.at[0 : nh // CORES - 1], wo_sem.at[1])
    for d in range(1, nh // CORES):
        src = (head + CORES * d) % nh
        remote(wo0.at[src], wo0.at[src], wo_sem.at[0], wo_sem.at[2], sibling).start()
    send_attended(0)
    kv_point(3)
    drain(wo0.at[0 : nh // CORES], wo_sem.at[2])
    for p in range(PARTS):
        gated = normed(0, p)
        full = wo0[...].reshape(nh * LANES, nh * LANES)
        for b in range(0, nh, 2):
            branch = dot(gated, full[:, b * LANES : (b + 2) * LANES])
            for e in range(2):
                hid[p, core, b + e] = (
                    hid0[p, core, b + e].astype(F32) + branch[:, e * LANES : (e + 1) * LANES]
                ).astype(BF16)
        remote(hid.at[p, core], hid.at[p, core], hid_ss, hid_rs.at[p], sibling).start()
    kv_point(4)
    for p in range(PARTS):
        drain(hid.at[p, 0], hid_rs.at[p])
        project(1, p, hid)
    kv_point(5)
    send_gates(1)
    for d in range(1, nh):
        remote(wo1_s.at[((head + d) % nh) // CORES], wo1.at[head], wt_sem.at[0], wt_sem.at[1], h_peer(d)).start()
    attention(1)
    send_attended(1)
    drain(wo1.at[0 : nh - 1], wt_sem.at[1])
    for p in range(PARTS):
        gated = normed(1, p)

        def final(c):
            branch = dot(gated, wo1[:, c].reshape(nh * LANES, LANES))
            return (hid[p, core, chip * CORES + c].astype(F32) + branch).astype(BF16)

        last_s[p] = final(1 - core)
        remote(last_s.at[p], last_r.at[p], last_sem.at[0], last_sem.at[1], sibling).start()
        out_ref[part_rows(p, core)] = final(core)

    drain(hid0.at[:, 0, 0 : nh - 1], tok_ss)
    drain(hid0.at[:, 0], fwd_ss)
    drain(wo0.at[0 : nh - 1], wo_sem.at[0])
    drain(wo1.at[0 : nh - 1], wt_sem.at[0])
    drain(hid.at[:, 0], hid_ss)
    for layer in range(LAYERS):
        drain(stay_s.at[layer], stay_ss.at[layer])
        drain(pair_s.at[layer], pair_ss.at[layer])
        if steps > 1:
            drain(q_all.at[layer, :, 0 : steps - 1], q_ss.at[layer])
            drain(part_s.at[layer], p_ss.at[layer])
        drain(gate_all.at[layer, :, 0 : nh - 1], g_ss.at[layer])
        drain(att_all.at[layer, :, 0 : nh - 1], a_ss.at[layer])
    drain(last_r, last_sem.at[1])
    drain(last_s, last_sem.at[0])
    for p in range(PARTS):
        out_ref[part_rows(p, 1 - core)] = last_r[p]


def body(x_size, nc, nh, tokens, request_user, hist_len, history, w_in, w_out):
    nx = x_size
    nz = nc // nx
    steps = nz // 2
    rows = tokens.shape[0] // PARTS
    half = rows // CORES
    users, events = history.shape[1], history.shape[2]
    width = nh * LANES
    hbm = pl.BlockSpec(memory_space=pltpu.HBM)
    smem = pl.BlockSpec(memory_space=pltpu.SMEM)
    sem = pltpu.SemaphoreType.DMA
    vmem = pltpu.VMEM
    return pl.pallas_call(
        functools.partial(kernel, (nz, nx, nh)),
        out_shape=jax.ShapeDtypeStruct((tokens.shape[0], LANES), BF16),
        in_specs=[smem, smem, hbm, hbm, hbm, hbm],
        out_specs=pl.BlockSpec(memory_space=pltpu.VMEM),
        scratch_shapes=[
            vmem((users, events, 2 * LANES), BF16),
            vmem((users, events, 2 * LANES), BF16),
            vmem((users, 2, events, LANES), BF16),
            vmem((users, 2, events, LANES), BF16),
            vmem((LAYERS, nx - 1, steps, 2, events, LANES), BF16),
            vmem((LAYERS, nx, steps, 2, events, LANES), BF16),
            vmem((LAYERS, nx, 2, steps, events, LANES), BF16),
            vmem((LAYERS, nx, 2, steps, events, LANES), BF16),
            vmem((PARTS * rows, LANES), BF16),
            vmem((PARTS, CORES, nh, half, LANES), BF16),
            vmem((PARTS, CORES, nh, half, LANES), BF16),
            vmem((nh, half, LANES), F32),
            vmem((LAYERS, width, 2 * LANES), BF16),
            vmem((nh, LANES, width), BF16),
            vmem((LAYERS, LANES, width), BF16),
            vmem((nh // CORES, CORES, LANES, LANES), BF16),
            vmem((nh, CORES, LANES, LANES), BF16),
            vmem((LAYERS, PARTS, steps, rows, LANES), BF16),
            vmem((LAYERS, PARTS, CORES, half, LANES), BF16),
            vmem((LAYERS, PARTS, nh, half, LANES), BF16),
            vmem((LAYERS, PARTS, max(steps - 1, 1), rows + EXTRA, LANES), BF16),
            vmem((LAYERS, PARTS, max(steps - 1, 1), rows + EXTRA, LANES), BF16),
            vmem((LAYERS, PARTS, CORES, half + EXTRA, LANES), BF16),
            vmem((LAYERS, PARTS, nh, half + EXTRA, LANES), BF16),
            vmem((PARTS, rows, LANES), F32),
            vmem((PARTS, 8, rows), F32),
            vmem((PARTS, half, LANES), BF16),
            vmem((PARTS, half, LANES), BF16),
            sem((5,)),
            sem, sem((PARTS,)), sem, sem((PARTS,)),
            sem((LAYERS,)), sem((LAYERS, steps)),
            sem((LAYERS,)), sem((LAYERS, steps)),
            sem((LAYERS,)), sem((LAYERS, PARTS, steps)),
            sem((LAYERS,)), sem((LAYERS, PARTS)),
            sem((LAYERS,)), sem((LAYERS, PARTS)),
            sem((LAYERS,)), sem((LAYERS, PARTS)),
            sem((3,)), sem((2,)),
            sem, sem((PARTS,)), sem((2,)),
        ],
        compiler_params=pltpu.CompilerParams(
            collective_id=0, has_side_effects=True, vmem_limit_bytes=60 * 1024 * 1024
        ),
    )(request_user.reshape(-1), hist_len, tokens, history, w_in, w_out)


def solution(mesh):
    in_specs = (
        P("cache", "head"),
        P(),
        P(),
        P(None, None, "cache", "head"),
        P(None, None, "head"),
        P(None, "head", None),
    )
    run = functools.partial(body, X_SIZE, mesh.shape["cache"], mesh.shape["head"])
    return jax.shard_map(run, mesh=mesh, in_specs=in_specs, out_specs=P("cache", "head"), check_vma=False)
```

```python
import functools

import jax
import jax.numpy as jnp
from jax import lax
from jax.experimental import pallas as pl
from jax.experimental.pallas import tpu as pltpu
from jax.sharding import PartitionSpec as P

DH = 64
LAYERS = 2
LANES = 128
X_SIZE = 4
CORES = 2
PARTS = 2
FIRST = (2, 1, 3)
ORDER = (((2, -1), (1, -1), (3, -1), (0, -1)), ((2, -1), (0, -1), (1, -1), (3, -1)))
EXTRA = 16
OWN, NEAR = True, False
PACE = (
    ((0, OWN, (2, 1, 3, 0)), (0, NEAR, (2, 1, 3, 0))), ((1, OWN, (2, 0, 1, 3)),), ((1, NEAR, (2, 0, 1, 3)),), (), (), (),
)
MESH = pl.DeviceIdType.MESH
F32 = jnp.float32
BF16 = jnp.bfloat16


def dot(a, b, dims=((1,), (0,))):
    return lax.dot_general(a, b, (dims, ((), ())), preferred_element_type=F32)


def silu(v):
    half = v * 0.5
    return half + half * jnp.tanh(half)


def lane_halves(rows):
    return lax.broadcasted_iota(jnp.int32, (rows, LANES), 1) < DH


def head_rows(value, dtype):
    row = lax.broadcasted_iota(jnp.int32, (8, LANES), 0)
    lane = lax.broadcasted_iota(jnp.int32, (8, LANES), 1)
    own = ((row == 0) & (lane < DH)) | ((row == 1) & (lane >= DH))
    return jnp.where(own, value, 0.0).astype(dtype)


def spread(flat):
    pick = head_rows(1.0, F32)
    if flat.shape[0] == 16:
        pick = jnp.concatenate([pick, pick], axis=0)
    return dot(flat, pick.astype(BF16), ((0,), (0,)))


def centre(block):
    return dot(head_rows(1.0 / DH, BF16), block.astype(BF16), ((1,), (1,))).astype(BF16)


def kernel(
    sizes, req_ref, len_ref, tok_hbm, hist_hbm, w_in_hbm, w_out_hbm, out_ref,
    raw0, raw1, hist0, hist1, stay_s, stay, pair_s, pair, own_tok, hid0, hid, hid_f, w_in, wo0, wo_own, wo1_s, wo1,
    q_all, gate_s, gate_all, part_s, part_r, att_s, att_all, acc, mid, last_s, last_r,
    load_sem, tok_ss, tok_rs, fwd_ss, fwd_rs, stay_ss, stay_rs, pair_ss, pair_rs, q_ss, q_rs, p_ss, p_rs, g_ss, g_rs, a_ss, a_rs, wo_sem, wt_sem,
    hid_ss, hid_rs, last_sem,
):
    nz, nx, nh = sizes
    steps = nz // 2
    users, events = raw0.shape[0], raw0.shape[1]
    half = hid0.shape[3]
    rows = CORES * half
    raws, hists = (raw0, raw1), (hist0, hist1)
    cache, head = lax.axis_index("cache"), lax.axis_index("head")
    z, x = cache // nx, cache % nx
    chip, core = head // CORES, head % CORES
    side = 1 - 2 * (z % 2)

    def part_rows(p, c):
        return pl.ds(pl.multiple_of(p * rows + c * half, half), half)

    def at(d_z, d_x):
        return (((z + d_z + nz) % nz) * nx + (x + d_x) % nx, head)

    def h_peer(d):
        return (cache, (head + d) % nh)

    sibling = (cache, head + 1 - 2 * core)

    def remote(src, dst, send, recv, device):
        return pltpu.make_async_remote_copy(
            src_ref=src, dst_ref=dst, send_sem=send, recv_sem=recv, device_id=device, device_id_type=MESH
        )

    def drain(ref, sem):
        pltpu.make_async_copy(ref, ref, sem).wait()

    loads = [
        pltpu.make_async_copy(hist_hbm.at[0], raw0, load_sem.at[0]),
        pltpu.make_async_copy(tok_hbm, own_tok, load_sem.at[1]),
        pltpu.make_async_copy(hist_hbm.at[1], raw1, load_sem.at[2]),
        pltpu.make_async_copy(w_in_hbm, w_in, load_sem.at[3]),
        pltpu.make_async_copy(w_out_hbm, wo_own, load_sem.at[4]),
    ]
    for load in loads:
        load.start()

    barrier = pltpu.get_barrier_semaphore()
    peers = [at(0, d) for d in range(1, nx)] + [h_peer(d) for d in range(1, nh)]
    peers += [at(2 * k, 0) for k in range(1, steps)]
    peers += [at(s, d) for s in (1, -1) for d in range(nx)]
    for peer in peers:
        pl.semaphore_signal(barrier, inc=1, device_id=peer, device_id_type=MESH)

    def prepare(layer):
        def one(u, carry):
            live = len_ref[u] - cache * events
            mask = lax.broadcasted_iota(jnp.int32, (events, LANES), 0) < live
            left = pltpu.roll(raws[layer][u, :, 0:LANES].astype(F32), DH, 1)
            right = raws[layer][u, :, LANES : 2 * LANES].astype(F32)
            hists[layer][u, 0] = jnp.where(mask, left, 0.0).astype(BF16)
            hists[layer][u, 1] = jnp.where(mask, right, 0.0).astype(BF16)
            return carry

        lax.fori_loop(0, users, one, 0)

    def gather(layer):
        def one(k, carry):
            for d in range(nx):
                to_x = (x + d) % nx
                block = hists[layer][req_ref[((z + 2 * k) % nz) * nx + to_x]]
                if d == 0:
                    stay[layer, x, k] = block
                else:
                    stay_s[layer, d - 1, k] = block
                for j in range(2):
                    to_z = (z + side * (1 - 2 * j) + 2 * k + nz) % nz
                    pair_s[layer, d, j, k] = hists[layer][req_ref[to_z * nx + to_x], j]
            return carry

        lax.fori_loop(0, steps, one, 0)

    def kv_send(layer, own, g):
        span = pl.ds(g, 1)
        for d in range(nx):
            if own and d:
                remote(
                    stay_s.at[layer, d - 1, span], stay.at[layer, x, span],
                    stay_ss.at[layer], stay_rs.at[layer, g], at(0, d),
                ).start()
            for j in range(0 if own else 2):
                remote(
                    pair_s.at[layer, d, j, span], pair.at[layer, x, j, span],
                    pair_ss.at[layer], pair_rs.at[layer, g], at(side * (1 - 2 * j), d),
                ).start()

    def kv_point(point):
        for layer, own, batch in PACE[point]:
            for g in batch:
                if g < steps:
                    kv_send(layer, own, g)

    def kv_wait(layer, g):
        span = pl.ds(g, 1)
        drain(stay.at[layer, 0 : nx - 1, span], stay_rs.at[layer, g])
        drain(pair.at[layer, :, :, span], pair_rs.at[layer, g])

    loads[0].wait()
    prepare(0)
    gather(0)
    loads[1].wait()
    for p in range(PARTS):
        hid0[p, core, head] = own_tok[part_rows(p, core)]
    pl.semaphore_wait(barrier, len(peers))
    for p in range(PARTS):
        for d in range(1, nh):
            to = (head + d) % CORES
            remote(own_tok.at[part_rows(p, to)], hid0.at[p, to, head], tok_ss, tok_rs.at[p], h_peer(d)).start()
    loads[4].wait()
    wo0[head] = wo_own[0]
    for d in range(1, nh // CORES):
        remote(wo0.at[head], wo0.at[head], wo_sem.at[0], wo_sem.at[1], h_peer(CORES * d)).start()
    remote(wo0.at[head], wo0.at[head], wo_sem.at[0], wo_sem.at[2], sibling).start()
    kv_point(0)
    loads[2].wait()
    prepare(1)
    gather(1)
    loads[3].wait()
    for b in range(nh):
        wo1_s[b // CORES, b % CORES] = wo_own[1, :, b * LANES : (b + 1) * LANES]
    wo1[head] = wo1_s[chip]

    def project(layer, p, halves):
        hidden = jnp.concatenate([halves[p, :, b].reshape(rows, LANES) for b in range(nh)], axis=1)
        left = silu(dot(hidden, w_in[layer, :, 0:LANES]))
        right = pltpu.roll(silu(dot(hidden, w_in[layer, :, LANES : 2 * LANES])), DH, 1)
        low = lane_halves(rows)
        q = (jnp.where(low, right, left).astype(BF16).astype(F32) * (0.5 * DH**-0.5)).astype(BF16)
        gates = jnp.where(low, left, right).astype(BF16)
        q_all[layer, p, 0] = q
        for c in range(CORES):
            gate_s[layer, p, c] = gates[c * half : (c + 1) * half]
        for k in [k for k in FIRST if k < steps]:
            remote(
                q_all.at[layer, p, 0], q_all.at[layer, p, steps - k],
                q_ss.at[layer], q_rs.at[layer, p, steps - k], at(2 * k, 0),
            ).start()

    def send_gates(layer):
        for p in range(PARTS):
            gate_all[layer, p, head] = gate_s[layer, p, core]
            for d in range(1, nh):
                remote(
                    gate_s.at[layer, p, (head + d) % CORES], gate_all.at[layer, p, head],
                    g_ss.at[layer], g_rs.at[layer, p], h_peer(d),
                ).start()

    def attend(layer, k, q):
        low = lane_halves(q.shape[0])
        zero = jnp.zeros_like(q)
        outs = []
        for j, q_one in ((0, jnp.where(low, zero, q)), (1, jnp.where(low, q, zero))):
            kvs, weights = [], []
            for s in range(0, nx, 2):
                for keys in (stay[layer, s : s + 2, k, j], pair[layer, s : s + 2, j, k]):
                    kv = keys.reshape(2 * events, LANES)
                    t = dot(q_one, kv, ((1,), (1,)))
                    kvs.append(kv)
                    weights.append((t + t * jnp.tanh(t)).astype(BF16))
            outs.append(dot(jnp.concatenate(weights, axis=1), jnp.concatenate(kvs, axis=0)))
        block = jnp.where(low, outs[0], outs[1])
        centres = centre(block)
        return block - spread(centres), centres.astype(F32)

    def give(layer, k, p, block, centres):
        part_s[layer, p, k - 1, 0:rows] = block.astype(BF16)
        part_s[layer, p, k - 1, rows : rows + EXTRA] = jnp.concatenate(
            [centres, jnp.zeros_like(centres)], axis=0
        ).astype(BF16)
        remote(
            part_s.at[layer, p, k - 1], part_r.at[layer, p, k - 1], p_ss.at[layer], p_rs.at[layer, p], at(2 * k, 0)
        ).start()

    def both(layer, k):
        q = jnp.concatenate([q_all[layer, p, k] for p in range(PARTS)], axis=0)
        block, centres = attend(layer, k, q)
        return [(block[p * rows : (p + 1) * rows], centres[:, p * rows : (p + 1) * rows]) for p in range(PARTS)]

    def forward_w_out():
        if nh > CORES:
            drain(wo0.at[0 : nh // CORES - 1], wo_sem.at[1])
        for d in range(1, nh // CORES):
            src = (head + CORES * d) % nh
            remote(wo0.at[src], wo0.at[src], wo_sem.at[0], wo_sem.at[2], sibling).start()

    def attention(layer):
        def own():
            kv_wait(layer, 0)
            for p, (block, centres) in enumerate(both(layer, 0)):
                acc[p] = block
                mid[p] = centres

        waited = [0]
        for k, p in ORDER[layer]:
            if k == 0:
                if layer == 0:
                    kv_point(2)
                own()
            elif k < steps:
                if k not in waited:
                    kv_wait(layer, k)
                    waited.append(k)
                for e in range(PARTS) if p < 0 else (p,):
                    drain(q_all.at[layer, e, k], q_rs.at[layer, e, k])
                if p < 0:
                    for e, (block, centres) in enumerate(both(layer, k)):
                        give(layer, k, e, block, centres)
                else:
                    give(layer, k, p, *attend(layer, k, q_all[layer, p, k]))

    def send_attended(layer):
        for p in range(PARTS):
            block, centres = acc[p], mid[p]
            if steps > 1:
                drain(part_r.at[layer, p], p_rs.at[layer, p])
            for k in range(steps - 1):
                block = block + part_r[layer, p, k, 0:rows].astype(F32)
                centres = centres + part_r[layer, p, k, rows : rows + EXTRA].astype(F32)[0:8]
            high = centres.astype(BF16).astype(F32)
            pairs = jnp.concatenate([high, centres - high], axis=0)
            for c in range(CORES):
                att_s[layer, p, c, 0:half] = block[c * half : (c + 1) * half].astype(BF16)
                shifted = pairs if c == 0 else pltpu.roll(pairs, rows - c * half, 1)
                att_s[layer, p, c, half : half + EXTRA] = shifted.astype(BF16)
            for d in range(1, nh):
                remote(
                    att_s.at[layer, p, (head + d) % CORES], att_all.at[layer, p, head],
                    a_ss.at[layer], a_rs.at[layer, p], h_peer(d),
                ).start()
            att_all[layer, p, head] = att_s[layer, p, core]

    def normed(layer, p):
        total = jnp.zeros((half, LANES), F32)
        squares = jnp.zeros((half, LANES), F32)
        drain(gate_all.at[layer, p, 0 : nh - 1], g_rs.at[layer, p])
        drain(att_all.at[layer, p, 0 : nh - 1], a_rs.at[layer, p])
        for b in range(nh):
            block = att_all[layer, p, b, 0:half].astype(F32) + spread(
                att_all[layer, p, b, half : half + EXTRA][:, 0:half]
            )
            hid_f[b] = block
            total = total + block
            squares = squares + block * block
        width = nh * LANES
        mean = jnp.sum(total, axis=1, keepdims=True) * (1.0 / width)
        var = jnp.sum(squares, axis=1, keepdims=True) * (1.0 / width) - mean * mean
        scale = lax.rsqrt(var + 1e-05)
        return jnp.concatenate(
            [((hid_f[b] - mean) * scale * gate_all[layer, p, b].astype(F32)).astype(BF16) for b in range(nh)], axis=1
        )

    for p in range(PARTS):
        drain(hid0.at[p, 0, 0 : nh - 1], tok_rs.at[p])
        remote(hid0.at[p, core], hid0.at[p, core], fwd_ss, fwd_rs.at[p], sibling).start()
    for p in range(PARTS):
        drain(hid0.at[p, 0], fwd_rs.at[p])
        project(0, p, hid0)
    kv_point(1)
    send_gates(0)
    forward_w_out()
    attention(0)
    send_attended(0)
    kv_point(3)
    drain(wo0.at[0 : nh // CORES], wo_sem.at[2])
    for p in range(PARTS):
        gated = normed(0, p)
        full = wo0[...].reshape(nh * LANES, nh * LANES)
        for b in range(0, nh, 2):
            branch = dot(gated, full[:, b * LANES : (b + 2) * LANES])
            for e in range(2):
                hid[p, core, b + e] = (
                    hid0[p, core, b + e].astype(F32) + branch[:, e * LANES : (e + 1) * LANES]
                ).astype(BF16)
        remote(hid.at[p, core], hid.at[p, core], hid_ss, hid_rs.at[p], sibling).start()
    kv_point(4)
    for p in range(PARTS):
        drain(hid.at[p, 0], hid_rs.at[p])
        project(1, p, hid)
    kv_point(5)
    send_gates(1)
    for d in range(1, nh):
        remote(wo1_s.at[((head + d) % nh) // CORES], wo1.at[head], wt_sem.at[0], wt_sem.at[1], h_peer(d)).start()
    attention(1)
    send_attended(1)
    drain(wo1.at[0 : nh - 1], wt_sem.at[1])
    for p in range(PARTS):
        gated = normed(1, p)

        def final(c):
            branch = dot(gated, wo1[:, c].reshape(nh * LANES, LANES))
            return (hid[p, core, chip * CORES + c].astype(F32) + branch).astype(BF16)

        last_s[p] = final(1 - core)
        remote(last_s.at[p], last_r.at[p], last_sem.at[0], last_sem.at[1], sibling).start()
        out_ref[part_rows(p, core)] = final(core)

    drain(hid0.at[:, 0, 0 : nh - 1], tok_ss)
    drain(hid0.at[:, 0], fwd_ss)
    drain(wo0.at[0 : nh - 1], wo_sem.at[0])
    drain(wo1.at[0 : nh - 1], wt_sem.at[0])
    drain(hid.at[:, 0], hid_ss)
    for layer in range(LAYERS):
        drain(stay_s.at[layer], stay_ss.at[layer])
        drain(pair_s.at[layer], pair_ss.at[layer])
        if steps > 1:
            drain(q_all.at[layer, :, 0 : steps - 1], q_ss.at[layer])
            drain(part_s.at[layer], p_ss.at[layer])
        drain(gate_all.at[layer, :, 0 : nh - 1], g_ss.at[layer])
        drain(att_all.at[layer, :, 0 : nh - 1], a_ss.at[layer])
    drain(last_r, last_sem.at[1])
    drain(last_s, last_sem.at[0])
    for p in range(PARTS):
        out_ref[part_rows(p, 1 - core)] = last_r[p]


def body(x_size, nc, nh, tokens, request_user, hist_len, history, w_in, w_out):
    nx = x_size
    nz = nc // nx
    steps = nz // 2
    rows = tokens.shape[0] // PARTS
    half = rows // CORES
    users, events = history.shape[1], history.shape[2]
    width = nh * LANES
    hbm = pl.BlockSpec(memory_space=pltpu.HBM)
    smem = pl.BlockSpec(memory_space=pltpu.SMEM)
    sem = pltpu.SemaphoreType.DMA
    vmem = pltpu.VMEM
    return pl.pallas_call(
        functools.partial(kernel, (nz, nx, nh)),
        out_shape=jax.ShapeDtypeStruct((tokens.shape[0], LANES), BF16),
        in_specs=[smem, smem, hbm, hbm, hbm, hbm],
        out_specs=pl.BlockSpec(memory_space=pltpu.VMEM),
        scratch_shapes=[
            vmem((users, events, 2 * LANES), BF16),
            vmem((users, events, 2 * LANES), BF16),
            vmem((users, 2, events, LANES), BF16),
            vmem((users, 2, events, LANES), BF16),
            vmem((LAYERS, nx - 1, steps, 2, events, LANES), BF16),
            vmem((LAYERS, nx, steps, 2, events, LANES), BF16),
            vmem((LAYERS, nx, 2, steps, events, LANES), BF16),
            vmem((LAYERS, nx, 2, steps, events, LANES), BF16),
            vmem((PARTS * rows, LANES), BF16),
            vmem((PARTS, CORES, nh, half, LANES), BF16),
            vmem((PARTS, CORES, nh, half, LANES), BF16),
            vmem((nh, half, LANES), F32),
            vmem((LAYERS, width, 2 * LANES), BF16),
            vmem((nh, LANES, width), BF16),
            vmem((LAYERS, LANES, width), BF16),
            vmem((nh // CORES, CORES, LANES, LANES), BF16),
            vmem((nh, CORES, LANES, LANES), BF16),
            vmem((LAYERS, PARTS, steps, rows, LANES), BF16),
            vmem((LAYERS, PARTS, CORES, half, LANES), BF16),
            vmem((LAYERS, PARTS, nh, half, LANES), BF16),
            vmem((LAYERS, PARTS, max(steps - 1, 1), rows + EXTRA, LANES), BF16),
            vmem((LAYERS, PARTS, max(steps - 1, 1), rows + EXTRA, LANES), BF16),
            vmem((LAYERS, PARTS, CORES, half + EXTRA, LANES), BF16),
            vmem((LAYERS, PARTS, nh, half + EXTRA, LANES), BF16),
            vmem((PARTS, rows, LANES), F32),
            vmem((PARTS, 8, rows), F32),
            vmem((PARTS, half, LANES), BF16),
            vmem((PARTS, half, LANES), BF16),
            sem((5,)),
            sem, sem((PARTS,)), sem, sem((PARTS,)),
            sem((LAYERS,)), sem((LAYERS, steps)),
            sem((LAYERS,)), sem((LAYERS, steps)),
            sem((LAYERS,)), sem((LAYERS, PARTS, steps)),
            sem((LAYERS,)), sem((LAYERS, PARTS)),
            sem((LAYERS,)), sem((LAYERS, PARTS)),
            sem((LAYERS,)), sem((LAYERS, PARTS)),
            sem((3,)), sem((2,)),
            sem, sem((PARTS,)), sem((2,)),
        ],
        compiler_params=pltpu.CompilerParams(
            collective_id=0, has_side_effects=True, vmem_limit_bytes=60 * 1024 * 1024
        ),
    )(request_user.reshape(-1), hist_len, tokens, history, w_in, w_out)


def solution(mesh):
    in_specs = (
        P("cache", "head"),
        P(),
        P(),
        P(None, None, "cache", "head"),
        P(None, None, "head"),
        P(None, "head", None),
    )
    run = functools.partial(body, X_SIZE, mesh.shape["cache"], mesh.shape["head"])
    return jax.shard_map(run, mesh=mesh, in_specs=in_specs, out_specs=P("cache", "head"), check_vma=False)
```

```python
import functools

import jax
import jax.numpy as jnp
from jax import lax
from jax.experimental import pallas as pl
from jax.experimental.pallas import tpu as pltpu
from jax.sharding import PartitionSpec as P

DH = 64
LAYERS = 2
LANES = 128
X_SIZE = 4
CORES = 2
PARTS = 2
FIRST = (2, 1, 3)
ORDER = (
    ((2, -1), (1, -1), (3, -1), (0, -1)), ((2, 0), (0, -1), (1, 0), (3, 0), (2, 1), (1, 1), (3, 1)),
)
EXTRA = 16
OWN, NEAR = True, False
PACE = (
    ((0, OWN, (2, 1, 3, 0)), (0, NEAR, (2, 1, 3, 0))), ((1, OWN, (2, 0, 1, 3)),), ((1, NEAR, (2, 0, 1, 3)),), (), (), (),
)
MESH = pl.DeviceIdType.MESH
F32 = jnp.float32
BF16 = jnp.bfloat16


def dot(a, b, dims=((1,), (0,))):
    return lax.dot_general(a, b, (dims, ((), ())), preferred_element_type=F32)


def silu(v):
    half = v * 0.5
    return half + half * jnp.tanh(half)


def lane_halves(rows):
    return lax.broadcasted_iota(jnp.int32, (rows, LANES), 1) < DH


def head_rows(value, dtype):
    row = lax.broadcasted_iota(jnp.int32, (8, LANES), 0)
    lane = lax.broadcasted_iota(jnp.int32, (8, LANES), 1)
    own = ((row == 0) & (lane < DH)) | ((row == 1) & (lane >= DH))
    return jnp.where(own, value, 0.0).astype(dtype)


def spread(flat):
    pick = head_rows(1.0, F32)
    if flat.shape[0] == 16:
        pick = jnp.concatenate([pick, pick], axis=0)
    return dot(flat, pick.astype(BF16), ((0,), (0,)))


def centre(block):
    return dot(head_rows(1.0 / DH, BF16), block.astype(BF16), ((1,), (1,))).astype(BF16)


def kernel(
    sizes, req_ref, len_ref, tok_hbm, hist_hbm, w_in_hbm, w_out_hbm, out_ref,
    raw0, raw1, hist0, hist1, stay_s, stay, pair_s, pair, own_tok, hid0, hid, hid_f, w_in, wo0, wo_own, wo1_s, wo1,
    q_all, gate_s, gate_all, part_s, part_r, att_s, att_all, acc, mid, last_s, last_r,
    load_sem, tok_ss, tok_rs, fwd_ss, fwd_rs, stay_ss, stay_rs, pair_ss, pair_rs, q_ss, q_rs, p_ss, p_rs, g_ss, g_rs, a_ss, a_rs, wo_sem, wt_sem,
    hid_ss, hid_rs, last_sem,
):
    nz, nx, nh = sizes
    steps = nz // 2
    users, events = raw0.shape[0], raw0.shape[1]
    half = hid0.shape[3]
    rows = CORES * half
    raws, hists = (raw0, raw1), (hist0, hist1)
    cache, head = lax.axis_index("cache"), lax.axis_index("head")
    z, x = cache // nx, cache % nx
    chip, core = head // CORES, head % CORES
    side = 1 - 2 * (z % 2)

    def part_rows(p, c):
        return pl.ds(pl.multiple_of(p * rows + c * half, half), half)

    def at(d_z, d_x):
        return (((z + d_z + nz) % nz) * nx + (x + d_x) % nx, head)

    def h_peer(d):
        return (cache, (head + d) % nh)

    sibling = (cache, head + 1 - 2 * core)

    def remote(src, dst, send, recv, device):
        return pltpu.make_async_remote_copy(
            src_ref=src, dst_ref=dst, send_sem=send, recv_sem=recv, device_id=device, device_id_type=MESH
        )

    def drain(ref, sem):
        pltpu.make_async_copy(ref, ref, sem).wait()

    loads = [
        pltpu.make_async_copy(hist_hbm.at[0], raw0, load_sem.at[0]),
        pltpu.make_async_copy(tok_hbm, own_tok, load_sem.at[1]),
        pltpu.make_async_copy(hist_hbm.at[1], raw1, load_sem.at[2]),
        pltpu.make_async_copy(w_in_hbm, w_in, load_sem.at[3]),
        pltpu.make_async_copy(w_out_hbm, wo_own, load_sem.at[4]),
    ]
    for load in loads:
        load.start()

    barrier = pltpu.get_barrier_semaphore()
    peers = [at(0, d) for d in range(1, nx)] + [h_peer(d) for d in range(1, nh)]
    peers += [at(2 * k, 0) for k in range(1, steps)]
    peers += [at(s, d) for s in (1, -1) for d in range(nx)]
    for peer in peers:
        pl.semaphore_signal(barrier, inc=1, device_id=peer, device_id_type=MESH)

    def prepare(layer):
        def one(u, carry):
            live = len_ref[u] - cache * events
            mask = lax.broadcasted_iota(jnp.int32, (events, LANES), 0) < live
            left = pltpu.roll(raws[layer][u, :, 0:LANES].astype(F32), DH, 1)
            right = raws[layer][u, :, LANES : 2 * LANES].astype(F32)
            hists[layer][u, 0] = jnp.where(mask, left, 0.0).astype(BF16)
            hists[layer][u, 1] = jnp.where(mask, right, 0.0).astype(BF16)
            return carry

        lax.fori_loop(0, users, one, 0)

    def gather(layer):
        def one(k, carry):
            for d in range(nx):
                to_x = (x + d) % nx
                block = hists[layer][req_ref[((z + 2 * k) % nz) * nx + to_x]]
                if d == 0:
                    stay[layer, x, k] = block
                else:
                    stay_s[layer, d - 1, k] = block
                for j in range(2):
                    to_z = (z + side * (1 - 2 * j) + 2 * k + nz) % nz
                    pair_s[layer, d, j, k] = hists[layer][req_ref[to_z * nx + to_x], j]
            return carry

        lax.fori_loop(0, steps, one, 0)

    def kv_send(layer, own, g):
        span = pl.ds(g, 1)
        for d in range(nx):
            if own and d:
                remote(
                    stay_s.at[layer, d - 1, span], stay.at[layer, x, span],
                    stay_ss.at[layer], stay_rs.at[layer, g], at(0, d),
                ).start()
            for j in range(0 if own else 2):
                remote(
                    pair_s.at[layer, d, j, span], pair.at[layer, x, j, span],
                    pair_ss.at[layer], pair_rs.at[layer, g], at(side * (1 - 2 * j), d),
                ).start()

    def kv_point(point):
        for layer, own, batch in PACE[point]:
            for g in batch:
                if g < steps:
                    kv_send(layer, own, g)

    def kv_wait(layer, g):
        span = pl.ds(g, 1)
        drain(stay.at[layer, 0 : nx - 1, span], stay_rs.at[layer, g])
        drain(pair.at[layer, :, :, span], pair_rs.at[layer, g])

    loads[0].wait()
    prepare(0)
    gather(0)
    loads[1].wait()
    for p in range(PARTS):
        hid0[p, core, head] = own_tok[part_rows(p, core)]
    pl.semaphore_wait(barrier, len(peers))
    for p in range(PARTS):
        for d in range(1, nh):
            to = (head + d) % CORES
            remote(own_tok.at[part_rows(p, to)], hid0.at[p, to, head], tok_ss, tok_rs.at[p], h_peer(d)).start()
    loads[4].wait()
    wo0[head] = wo_own[0]
    for d in range(1, nh // CORES):
        remote(wo0.at[head], wo0.at[head], wo_sem.at[0], wo_sem.at[1], h_peer(CORES * d)).start()
    remote(wo0.at[head], wo0.at[head], wo_sem.at[0], wo_sem.at[2], sibling).start()
    kv_point(0)
    loads[2].wait()
    prepare(1)
    gather(1)
    loads[3].wait()
    for b in range(nh):
        wo1_s[b // CORES, b % CORES] = wo_own[1, :, b * LANES : (b + 1) * LANES]
    wo1[head] = wo1_s[chip]

    def project(layer, p, halves):
        hidden = jnp.concatenate([halves[p, :, b].reshape(rows, LANES) for b in range(nh)], axis=1)
        left = silu(dot(hidden, w_in[layer, :, 0:LANES]))
        right = pltpu.roll(silu(dot(hidden, w_in[layer, :, LANES : 2 * LANES])), DH, 1)
        low = lane_halves(rows)
        q = (jnp.where(low, right, left).astype(BF16).astype(F32) * (0.5 * DH**-0.5)).astype(BF16)
        gates = jnp.where(low, left, right).astype(BF16)
        q_all[layer, p, 0] = q
        for c in range(CORES):
            gate_s[layer, p, c] = gates[c * half : (c + 1) * half]
        for k in [k for k in FIRST if k < steps]:
            remote(
                q_all.at[layer, p, 0], q_all.at[layer, p, steps - k],
                q_ss.at[layer], q_rs.at[layer, p, steps - k], at(2 * k, 0),
            ).start()

    def send_gates(layer):
        for p in range(PARTS):
            gate_all[layer, p, head] = gate_s[layer, p, core]
            for d in range(1, nh):
                remote(
                    gate_s.at[layer, p, (head + d) % CORES], gate_all.at[layer, p, head],
                    g_ss.at[layer], g_rs.at[layer, p], h_peer(d),
                ).start()

    def attend(layer, k, q):
        low = lane_halves(q.shape[0])
        zero = jnp.zeros_like(q)
        outs = []
        for j, q_one in ((0, jnp.where(low, zero, q)), (1, jnp.where(low, q, zero))):
            kvs, weights = [], []
            for s in range(0, nx, 2):
                for keys in (stay[layer, s : s + 2, k, j], pair[layer, s : s + 2, j, k]):
                    kv = keys.reshape(2 * events, LANES)
                    t = dot(q_one, kv, ((1,), (1,)))
                    kvs.append(kv)
                    weights.append((t + t * jnp.tanh(t)).astype(BF16))
            outs.append(dot(jnp.concatenate(weights, axis=1), jnp.concatenate(kvs, axis=0)))
        block = jnp.where(low, outs[0], outs[1])
        centres = centre(block)
        return block - spread(centres), centres.astype(F32)

    def give(layer, k, p, block, centres):
        part_s[layer, p, k - 1, 0:rows] = block.astype(BF16)
        part_s[layer, p, k - 1, rows : rows + EXTRA] = jnp.concatenate(
            [centres, jnp.zeros_like(centres)], axis=0
        ).astype(BF16)
        remote(
            part_s.at[layer, p, k - 1], part_r.at[layer, p, k - 1], p_ss.at[layer], p_rs.at[layer, p], at(2 * k, 0)
        ).start()

    def both(layer, k):
        q = jnp.concatenate([q_all[layer, p, k] for p in range(PARTS)], axis=0)
        block, centres = attend(layer, k, q)
        return [(block[p * rows : (p + 1) * rows], centres[:, p * rows : (p + 1) * rows]) for p in range(PARTS)]

    def forward_w_out():
        if nh > CORES:
            drain(wo0.at[0 : nh // CORES - 1], wo_sem.at[1])
        for d in range(1, nh // CORES):
            src = (head + CORES * d) % nh
            remote(wo0.at[src], wo0.at[src], wo_sem.at[0], wo_sem.at[2], sibling).start()

    def attention(layer):
        def own():
            kv_wait(layer, 0)
            for p, (block, centres) in enumerate(both(layer, 0)):
                acc[p] = block
                mid[p] = centres

        waited = [0]
        for k, p in ORDER[layer]:
            if k == 0:
                if layer == 0:
                    kv_point(2)
                own()
            elif k < steps:
                if k not in waited:
                    kv_wait(layer, k)
                    waited.append(k)
                for e in range(PARTS) if p < 0 else (p,):
                    drain(q_all.at[layer, e, k], q_rs.at[layer, e, k])
                if p < 0:
                    for e, (block, centres) in enumerate(both(layer, k)):
                        give(layer, k, e, block, centres)
                else:
                    give(layer, k, p, *attend(layer, k, q_all[layer, p, k]))

    def send_attended(layer):
        for p in range(PARTS):
            block, centres = acc[p], mid[p]
            if steps > 1:
                drain(part_r.at[layer, p], p_rs.at[layer, p])
            for k in range(steps - 1):
                block = block + part_r[layer, p, k, 0:rows].astype(F32)
                centres = centres + part_r[layer, p, k, rows : rows + EXTRA].astype(F32)[0:8]
            high = centres.astype(BF16).astype(F32)
            pairs = jnp.concatenate([high, centres - high], axis=0)
            for c in range(CORES):
                att_s[layer, p, c, 0:half] = block[c * half : (c + 1) * half].astype(BF16)
                shifted = pairs if c == 0 else pltpu.roll(pairs, rows - c * half, 1)
                att_s[layer, p, c, half : half + EXTRA] = shifted.astype(BF16)
            for d in range(1, nh):
                remote(
                    att_s.at[layer, p, (head + d) % CORES], att_all.at[layer, p, head],
                    a_ss.at[layer], a_rs.at[layer, p], h_peer(d),
                ).start()
            att_all[layer, p, head] = att_s[layer, p, core]

    def normed(layer, p):
        total = jnp.zeros((half, LANES), F32)
        squares = jnp.zeros((half, LANES), F32)
        drain(gate_all.at[layer, p, 0 : nh - 1], g_rs.at[layer, p])
        drain(att_all.at[layer, p, 0 : nh - 1], a_rs.at[layer, p])
        for b in range(nh):
            block = att_all[layer, p, b, 0:half].astype(F32) + spread(
                att_all[layer, p, b, half : half + EXTRA][:, 0:half]
            )
            hid_f[b] = block
            total = total + block
            squares = squares + block * block
        width = nh * LANES
        mean = jnp.sum(total, axis=1, keepdims=True) * (1.0 / width)
        var = jnp.sum(squares, axis=1, keepdims=True) * (1.0 / width) - mean * mean
        scale = lax.rsqrt(var + 1e-05)
        return jnp.concatenate(
            [((hid_f[b] - mean) * scale * gate_all[layer, p, b].astype(F32)).astype(BF16) for b in range(nh)], axis=1
        )

    for p in range(PARTS):
        drain(hid0.at[p, 0, 0 : nh - 1], tok_rs.at[p])
        remote(hid0.at[p, core], hid0.at[p, core], fwd_ss, fwd_rs.at[p], sibling).start()
    for p in range(PARTS):
        drain(hid0.at[p, 0], fwd_rs.at[p])
        project(0, p, hid0)
    kv_point(1)
    send_gates(0)
    forward_w_out()
    attention(0)
    send_attended(0)
    kv_point(3)
    drain(wo0.at[0 : nh // CORES], wo_sem.at[2])
    for p in range(PARTS):
        gated = normed(0, p)
        full = wo0[...].reshape(nh * LANES, nh * LANES)
        for b in range(0, nh, 2):
            branch = dot(gated, full[:, b * LANES : (b + 2) * LANES])
            for e in range(2):
                hid[p, core, b + e] = (
                    hid0[p, core, b + e].astype(F32) + branch[:, e * LANES : (e + 1) * LANES]
                ).astype(BF16)
        remote(hid.at[p, core], hid.at[p, core], hid_ss, hid_rs.at[p], sibling).start()
    kv_point(4)
    for p in range(PARTS):
        drain(hid.at[p, 0], hid_rs.at[p])
        project(1, p, hid)
    kv_point(5)
    send_gates(1)
    for d in range(1, nh):
        remote(wo1_s.at[((head + d) % nh) // CORES], wo1.at[head], wt_sem.at[0], wt_sem.at[1], h_peer(d)).start()
    attention(1)
    send_attended(1)
    drain(wo1.at[0 : nh - 1], wt_sem.at[1])
    for p in range(PARTS):
        gated = normed(1, p)

        def final(c):
            branch = dot(gated, wo1[:, c].reshape(nh * LANES, LANES))
            return (hid[p, core, chip * CORES + c].astype(F32) + branch).astype(BF16)

        last_s[p] = final(1 - core)
        remote(last_s.at[p], last_r.at[p], last_sem.at[0], last_sem.at[1], sibling).start()
        out_ref[part_rows(p, core)] = final(core)

    drain(hid0.at[:, 0, 0 : nh - 1], tok_ss)
    drain(hid0.at[:, 0], fwd_ss)
    drain(wo0.at[0 : nh - 1], wo_sem.at[0])
    drain(wo1.at[0 : nh - 1], wt_sem.at[0])
    drain(hid.at[:, 0], hid_ss)
    for layer in range(LAYERS):
        drain(stay_s.at[layer], stay_ss.at[layer])
        drain(pair_s.at[layer], pair_ss.at[layer])
        if steps > 1:
            drain(q_all.at[layer, :, 0 : steps - 1], q_ss.at[layer])
            drain(part_s.at[layer], p_ss.at[layer])
        drain(gate_all.at[layer, :, 0 : nh - 1], g_ss.at[layer])
        drain(att_all.at[layer, :, 0 : nh - 1], a_ss.at[layer])
    drain(last_r, last_sem.at[1])
    drain(last_s, last_sem.at[0])
    for p in range(PARTS):
        out_ref[part_rows(p, 1 - core)] = last_r[p]


def body(x_size, nc, nh, tokens, request_user, hist_len, history, w_in, w_out):
    nx = x_size
    nz = nc // nx
    steps = nz // 2
    rows = tokens.shape[0] // PARTS
    half = rows // CORES
    users, events = history.shape[1], history.shape[2]
    width = nh * LANES
    hbm = pl.BlockSpec(memory_space=pltpu.HBM)
    smem = pl.BlockSpec(memory_space=pltpu.SMEM)
    sem = pltpu.SemaphoreType.DMA
    vmem = pltpu.VMEM
    return pl.pallas_call(
        functools.partial(kernel, (nz, nx, nh)),
        out_shape=jax.ShapeDtypeStruct((tokens.shape[0], LANES), BF16),
        in_specs=[smem, smem, hbm, hbm, hbm, hbm],
        out_specs=pl.BlockSpec(memory_space=pltpu.VMEM),
        scratch_shapes=[
            vmem((users, events, 2 * LANES), BF16),
            vmem((users, events, 2 * LANES), BF16),
            vmem((users, 2, events, LANES), BF16),
            vmem((users, 2, events, LANES), BF16),
            vmem((LAYERS, nx - 1, steps, 2, events, LANES), BF16),
            vmem((LAYERS, nx, steps, 2, events, LANES), BF16),
            vmem((LAYERS, nx, 2, steps, events, LANES), BF16),
            vmem((LAYERS, nx, 2, steps, events, LANES), BF16),
            vmem((PARTS * rows, LANES), BF16),
            vmem((PARTS, CORES, nh, half, LANES), BF16),
            vmem((PARTS, CORES, nh, half, LANES), BF16),
            vmem((nh, half, LANES), F32),
            vmem((LAYERS, width, 2 * LANES), BF16),
            vmem((nh, LANES, width), BF16),
            vmem((LAYERS, LANES, width), BF16),
            vmem((nh // CORES, CORES, LANES, LANES), BF16),
            vmem((nh, CORES, LANES, LANES), BF16),
            vmem((LAYERS, PARTS, steps, rows, LANES), BF16),
            vmem((LAYERS, PARTS, CORES, half, LANES), BF16),
            vmem((LAYERS, PARTS, nh, half, LANES), BF16),
            vmem((LAYERS, PARTS, max(steps - 1, 1), rows + EXTRA, LANES), BF16),
            vmem((LAYERS, PARTS, max(steps - 1, 1), rows + EXTRA, LANES), BF16),
            vmem((LAYERS, PARTS, CORES, half + EXTRA, LANES), BF16),
            vmem((LAYERS, PARTS, nh, half + EXTRA, LANES), BF16),
            vmem((PARTS, rows, LANES), F32),
            vmem((PARTS, 8, rows), F32),
            vmem((PARTS, half, LANES), BF16),
            vmem((PARTS, half, LANES), BF16),
            sem((5,)),
            sem, sem((PARTS,)), sem, sem((PARTS,)),
            sem((LAYERS,)), sem((LAYERS, steps)),
            sem((LAYERS,)), sem((LAYERS, steps)),
            sem((LAYERS,)), sem((LAYERS, PARTS, steps)),
            sem((LAYERS,)), sem((LAYERS, PARTS)),
            sem((LAYERS,)), sem((LAYERS, PARTS)),
            sem((LAYERS,)), sem((LAYERS, PARTS)),
            sem((3,)), sem((2,)),
            sem, sem((PARTS,)), sem((2,)),
        ],
        compiler_params=pltpu.CompilerParams(
            collective_id=0, has_side_effects=True, vmem_limit_bytes=60 * 1024 * 1024
        ),
    )(request_user.reshape(-1), hist_len, tokens, history, w_in, w_out)


def solution(mesh):
    in_specs = (
        P("cache", "head"),
        P(),
        P(),
        P(None, None, "cache", "head"),
        P(None, None, "head"),
        P(None, "head", None),
    )
    run = functools.partial(body, X_SIZE, mesh.shape["cache"], mesh.shape["head"])
    return jax.shard_map(run, mesh=mesh, in_specs=in_specs, out_specs=P("cache", "head"), check_vma=False)
```
